32 devices in a mesh: group: 2 (over y), dp: 4 (over z), tok: 4 (over x, core).
Axes of the slice: x: 2, y: 2, z: 4, core: 2. Of those that a mesh axis runs over, the one named last changes fastest.
Arguments:
- pre_norm: bfloat16 [384, 16, 1536], P(('group', 'dp'), 'tok'), parts along dimension 0, may hold values from -6 to 6
- cotangent: bfloat16 [384, 16, 1536], P(('group', 'dp'), 'tok'), parts along dimension 0, may hold values from -6 to 6
- gain: float32 [16, 1536], P('tok'), may hold values from 0.5 to 1.5
- pre_act: bfloat16 [384, 16, 6144], P('group', 'tok', 'dp'), parts along dimension 0, may hold values from -6 to 6
- gates: float32 [8, 16, 6144], P(None, 'tok', 'dp'), may hold values from 0.25 to 4
- down_weight: bfloat16 [16, 6144, 1536], P('tok', 'dp'), may hold values from -0.078125 to 0.078125
- scenario: int32 [384], P('group'), parts along dimension 0, may hold values from 0 to 7
Outputs:
- d_input: bfloat16 [384, 16, 1536], P(('group', 'dp'), 'tok'), parts along dimension 0
- d_pre_act: bfloat16 [384, 16, 6144], P('group', 'tok', 'dp'), parts along dimension 0
- d_down: bfloat16 [32, 6144, 1536], P(('group', 'tok'), 'dp'), parts along dimension 0
- d_gates: float32 [16, 16, 6144], P('group', 'tok', 'dp'), parts along dimension 0
- gain_gradient: float32 [32, 1536], P(('group', 'tok'), 'dp'), parts along dimension 0
The draws below stay inside these ranges and needn't reach their ends.
There are 2 independent parts, one for each index of `group`. The reference program is written for one: setup_inputs(seed, part) draws one part's arguments, and reference() takes and returns one part's arrays. A program takes and returns all parts, laid end to end along the dimension named above; an argument that names none is the same for every part. Nothing has to cross between parts.
All inputs are finite; a program needn't handle non-finite values.
Results may differ from the reference program's by a relative error of at most 0.0058.
Values may be sent and summed in bfloat16 or wider, within the bound.
No kernel may reach another device: no remote copies, remote signals or barrier semaphores. Data moves between devices by JAX's collectives and lax.ppermute only.
A program may use at most 128 MiB of HBM per device.

```python
import math
import jax
import jax.numpy as jnp
from jax import lax

D = 1536
FF = 6144
SCEN = 8
TOKS = 16
EX = 192
PIECE = 96


def plant(values, key, low, largest):
    index_at = [jax.random.randint(jax.random.fold_in(key, axis), (), 0, length) for axis, length in enumerate(values.shape)]
    main_axis = values.shape.index(max(values.shape))
    neighbour = index_at[:main_axis] + [(index_at[main_axis] + 1) % values.shape[main_axis]] + index_at[main_axis + 1:]
    return values.at[tuple(index_at)].set(low).at[tuple(neighbour)].set(largest)


def strengthened(drawn, stream_key, source, target, shards_of, factor):
    def block_of(axis_at):
        return (jnp.arange(drawn.shape[axis_at]) // (drawn.shape[axis_at] // shards_of)).reshape((-1,) + (1,) * (drawn.ndim - 1 - axis_at))

    near = jax.random.permutation(stream_key, shards_of)[block_of(target)]
    second = (block_of(target) + shards_of // 2) % shards_of
    return jnp.where((block_of(source) == near) | (block_of(source) == second), factor * drawn, drawn)


def shard_levels(own_key, shape, split, low, largest):
    level = 1.0
    for position, shards_of in split:
        heights = jax.random.uniform(jax.random.fold_in(jax.random.fold_in(own_key, 6), position), (shards_of,), jnp.float32, low / len(split), largest / len(split))
        level = level * jnp.repeat(jnp.exp(heights), shape[position] // shards_of).reshape((-1,) + (1,) * (len(shape) - 1 - position))
    return level


def scatter_about(stream_key, shape, scale, most, pieces=(), kind=jnp.bfloat16):
    loudness = shard_levels(stream_key, shape, pieces, -0.22, 0.18) if pieces else 1.0
    array = jax.random.normal(stream_key, shape, jnp.float32) * scale * loudness
    return jnp.minimum(jnp.maximum(array, -most), most).astype(kind)


def noise_with(stream_key, dims, deviation, most, cuts, heavy, kind=jnp.bfloat16):
    drawn = deviation * jax.random.normal(stream_key, dims, jnp.float32)
    if cuts:
        drawn = drawn * shard_levels(stream_key, dims, cuts, -0.22, 0.18)
    return jnp.clip(strengthened(drawn, jax.random.fold_in(stream_key, 3), *heavy), -most, most).astype(kind)


def setup_inputs(seed: int = 0, part: int = 0) -> dict:
    keys = jax.random.split(jax.random.key(seed), 8)
    part_splits = jax.random.split(jax.random.fold_in(keys[7], part), 8)
    pre_norm = scatter_about(part_splits[0], (EX, TOKS, D), 1.0, 6.0, ((0, 4), (1, 4)))
    cotangent = noise_with(part_splits[1], (EX, TOKS, D), 1.0, 6.0, ((0, 4), (1, 4)), (0, 2, 4, 2.0))
    gain = jnp.clip(1.0 + 0.1 * jax.random.normal(keys[2], (TOKS, D), jnp.float32), 0.5, 1.5)
    pre_act = scatter_about(part_splits[3], (EX, TOKS, FF), 1.0, 6.0, ((1, 4), (2, 4)))
    gates = jnp.clip(jnp.exp(math.log(4.0) - 2.7725887 * jax.random.uniform(keys[4], (SCEN, TOKS, FF), jnp.float32) ** shard_levels(keys[4], (SCEN, TOKS, FF), ((1, 4), (2, 4)), -0.2, 0.2)), 0.25, 4.0)
    down_weight = scatter_about(keys[5], (TOKS, FF, D), FF ** -0.5, 0.078125, ((0, 4), (1, 4)))
    scenario = plant(jax.random.randint(part_splits[6], (EX,), 0, SCEN), jax.random.fold_in(part_splits[6], 1), 0, SCEN - 1).astype(jnp.int32)
    return dict(pre_norm=pre_norm, cotangent=cotangent, gain=gain, pre_act=pre_act, gates=gates, down_weight=down_weight, scenario=scenario)


def gelu_parts(value):
    cubic = 0.7978845608 * (value + 0.044715 * value * value * value)
    tangent = jnp.tanh(cubic)
    activated = 0.5 * value * (1.0 + tangent)
    slope = 0.5 * (1.0 + tangent) + 0.5 * value * (1.0 - tangent * tangent) * 0.7978845608 * (1.0 + 3.0 * 0.044715 * value * value)
    return (activated, slope)

def mix_tokens(value):
    rows = value.shape[0]
    return value.reshape(rows, TOKS, TOKS, PIECE).transpose(0, 2, 1, 3).reshape(rows, TOKS, D)

def reference(pre_norm, cotangent, gain, pre_act, gates, down_weight, scenario):
    inputs = pre_norm.astype(jnp.float32)
    centered_rows = inputs - lax.optimization_barrier(jnp.mean(inputs, axis=-1, keepdims=True))
    inverse_deviation = lax.rsqrt(lax.optimization_barrier(jnp.mean(centered_rows * centered_rows, axis=-1, keepdims=True)) + 1e-05)
    normalized_input = centered_rows * inverse_deviation
    gradient_results = cotangent.astype(jnp.float32)
    gain_gradient = lax.optimization_barrier(jnp.sum(gradient_results * normalized_input, axis=0))
    scaled_gradient = gradient_results * gain
    norm_output_gradient = inverse_deviation * (scaled_gradient - lax.optimization_barrier(jnp.mean(scaled_gradient, axis=-1, keepdims=True)) - normalized_input * lax.optimization_barrier(jnp.mean(scaled_gradient * normalized_input, axis=-1, keepdims=True)))
    dz_b = norm_output_gradient.astype(jnp.bfloat16)
    d_input = (dz_b.astype(jnp.float32) + mix_tokens(dz_b).astype(jnp.float32)).astype(jnp.bfloat16)
    onehot = (scenario[:, None] == jnp.arange(SCEN, dtype=jnp.int32)[None, :]).astype(jnp.float32)
    pre_list, down_list, gate_list = ([], [], [])
    for token in range(TOKS):
        act = pre_act[:, token, :].astype(jnp.float32)
        activated, slope = gelu_parts(act)
        gate_rows = jnp.dot(onehot, gates[:, token, :], precision=lax.Precision.HIGHEST)
        hidden = (activated * gate_rows).astype(jnp.bfloat16)
        d_hidden = jnp.dot(dz_b[:, token, :], down_weight[token].T, preferred_element_type=jnp.float32)
        gate_list.append(jnp.dot(onehot.T, d_hidden * activated, precision=lax.Precision.HIGHEST))
        pre_list.append((d_hidden * gate_rows * slope).astype(jnp.bfloat16))
        down_list.append(jnp.dot(hidden.T, dz_b[:, token, :], preferred_element_type=jnp.float32).astype(jnp.bfloat16))
    d_pre_act = jnp.stack(pre_list, axis=1)
    d_down = jnp.stack(down_list, axis=0)
    d_gates = jnp.stack(gate_list, axis=1)
    return (d_input, d_pre_act, d_down, d_gates, gain_gradient)
```

```python
import functools
import jax
import jax.numpy as jnp
import numpy as np
from jax import lax
from jax.experimental import pallas as pl
from jax.experimental.pallas import tpu as pltpu
from jax.sharding import PartitionSpec as P

F32 = jnp.float32
BF16 = jnp.bfloat16
MIB = 1 << 20


def gelu_parts(value):
    square = value * value
    tangent = jnp.tanh(0.7978845608 * (value + 0.044715 * value * square))
    half = 0.5 * (1.0 + tangent)
    activated = value * half
    slope = half + 0.5 * value * (1.0 - tangent * tangent) * 0.7978845608 * (
        1.0 + 3.0 * 0.044715 * square
    )
    return activated, slope


def ring_order(count):
    return [0] + list(range(1, count, 2)) + list(range(2, count, 2))[::-1]


def take_rows(rows_ref, t, count, toks):
    return jnp.concatenate(
        [rows_ref[j, pl.ds(t, count, stride=toks), :] for j in range(rows_ref.shape[0])], axis=1
    )


def put_rows(rows_ref, t, count, toks, value, first=0):
    for j in range(value.shape[1] // 128):
        rows_ref[first + j, pl.ds(t, count, stride=toks), :] = value[:, j * 128 : (j + 1) * 128]


def spill(rows_ref, out_ref):
    count, toks, width = out_ref.shape
    for j in range(width // 128):
        out_ref[:, :, j * 128 : (j + 1) * 128] = (
            rows_ref[j].reshape(count, toks, 128).astype(out_ref.dtype)
        )


def norm_kernel(x_ref, g_ref, gain_ref, dz_ref, send_ref, gg_ref, rows_ref):
    count, toks, width = x_ref.shape
    step = 8 // toks
    gain = jnp.concatenate([gain_ref[...]] * step, axis=0)
    scale = 1.0 / width
    total = jnp.zeros((8, width), F32)
    for i in range(count // step):
        x = x_ref[i * step : (i + 1) * step].astype(F32).reshape(8, width)
        ct = g_ref[i * step : (i + 1) * step].astype(F32).reshape(8, width)
        g = ct * gain
        c = x - jnp.sum(x, axis=-1, keepdims=True) * scale
        mean_g = jnp.sum(g, axis=-1, keepdims=True) * scale
        rstd = lax.rsqrt(jnp.sum(c * c, axis=-1, keepdims=True) * scale + 1e-05)
        mean_gc = jnp.sum(g * c, axis=-1, keepdims=True) * scale
        xhat = c * rstd
        total = total + ct * xhat
        dz = rstd * (g - mean_g - xhat * (mean_gc * rstd))
        for j in range(width // 128):
            rows_ref[j, i * 8 : (i + 1) * 8, :] = dz[:, j * 128 : (j + 1) * 128]
    part = sum(total[k * toks : (k + 1) * toks] for k in range(step))
    owners, _, share = gg_ref.shape
    for p in range(owners):
        gg_ref[p] = part[:, p * share : (p + 1) * share]
    groups = send_ref.shape[0]
    block = width // groups
    for t in range(toks):
        row = take_rows(rows_ref, t, count, toks).astype(BF16)
        dz_ref[t] = row
        for p in range(groups):
            send_ref[p, t] = row[:, p * block : (p + 1) * block]


def norm(pre_norm, cotangent, gain, owners, groups):
    count, toks, width = pre_norm.shape
    return pl.pallas_call(
        norm_kernel,
        out_shape=(
            jax.ShapeDtypeStruct((toks, count, width), BF16),
            jax.ShapeDtypeStruct((groups, toks, count, width // groups), BF16),
            jax.ShapeDtypeStruct((owners, toks, width // owners), F32),
        ),
        in_specs=[pl.BlockSpec(memory_space=pltpu.VMEM)] * 3,
        out_specs=[pl.BlockSpec(memory_space=pltpu.VMEM)] * 3,
        scratch_shapes=[pltpu.VMEM((width // 128, count * toks, 128), F32)],
        compiler_params=pltpu.CompilerParams(vmem_limit_bytes=16 * MIB),
        name="norm",
    )(pre_norm, cotangent, gain)


def mix_kernel(recv_ref, dz_ref, out_ref, rows_ref):
    groups, toks, count, block = recv_ref.shape
    piece = block // toks
    for q in range(groups):
        got = [recv_ref[q, i].astype(F32) for i in range(toks)]
        for j in range(toks):
            mixed = jnp.concatenate(
                [got[i][:, j * piece : (j + 1) * piece] for i in range(toks)], axis=1
            )
            mixed = mixed + dz_ref[j, :, q * block : (q + 1) * block].astype(F32)
            put_rows(rows_ref, j, count, toks, mixed, q * block // 128)
    spill(rows_ref, out_ref)


def mix(recv, dz):
    toks, count, width = dz.shape
    return pl.pallas_call(
        mix_kernel,
        out_shape=jax.ShapeDtypeStruct((count, toks, width), BF16),
        in_specs=[pl.BlockSpec(memory_space=pltpu.VMEM)] * 2,
        out_specs=pl.BlockSpec(memory_space=pltpu.VMEM),
        scratch_shapes=[pltpu.VMEM((width // 128, count * toks, 128), F32)],
        compiler_params=pltpu.CompilerParams(vmem_limit_bytes=16 * MIB),
        name="mix",
    )(recv, dz)


def act_kernel(pre_ref, gates_ref, hot_ref, ht_ref, act_ref, mul_ref, rows_ref):
    count, toks, width = pre_ref.shape
    scen = gates_ref.shape[0]
    for j in range(width // 128):
        rows_ref[j] = (
            pre_ref[:, :, j * 128 : (j + 1) * 128].astype(F32).reshape(count * toks, 128)
        )
    hot = hot_ref[...]
    for t in range(toks):
        gate = gates_ref[:, t, :]
        high = gate.astype(BF16)
        rest = gate - high.astype(F32)
        mid = rest.astype(BF16)
        low = (rest - mid.astype(F32)).astype(BF16)
        rate = (
            jnp.dot(hot, high, preferred_element_type=F32)
            + jnp.dot(hot, mid, preferred_element_type=F32)
            + jnp.dot(hot, low, preferred_element_type=F32)
        )
        activated, slope = gelu_parts(take_rows(rows_ref, t, count, toks))
        ht_ref[t] = (activated * rate).T.astype(BF16)
        act_ref[t] = activated
        mul_ref[t] = rate * slope


def activations(pre_act, gates, hot, block):
    count, toks, width = pre_act.shape
    scen = gates.shape[0]
    return pl.pallas_call(
        act_kernel,
        grid=(width // block,),
        in_specs=[
            pl.BlockSpec((count, toks, block), lambda i: (0, 0, i)),
            pl.BlockSpec((scen, toks, block), lambda i: (0, 0, i)),
            pl.BlockSpec((count, scen), lambda i: (0, 0)),
        ],
        out_specs=[
            pl.BlockSpec((toks, block, count), lambda i: (0, i, 0)),
            pl.BlockSpec((toks, count, block), lambda i: (0, 0, i)),
            pl.BlockSpec((toks, count, block), lambda i: (0, 0, i)),
        ],
        out_shape=(
            jax.ShapeDtypeStruct((toks, width, count), BF16),
            jax.ShapeDtypeStruct((toks, count, width), F32),
            jax.ShapeDtypeStruct((toks, count, width), F32),
        ),
        scratch_shapes=[pltpu.VMEM((block // 128, count * toks, 128), F32)],
        compiler_params=pltpu.CompilerParams(vmem_limit_bytes=24 * MIB),
        cost_estimate=pl.CostEstimate(
            flops=30 * count * toks * width,
            bytes_accessed=12 * count * toks * width,
            transcendentals=count * toks * width,
        ),
        name="act",
    )(pre_act, gates, hot)


def token_kernel(parts, earlier, merge, idx_ref, *refs):
    shards, refs = refs[:parts], refs[parts:]
    w_ref, act_ref, mul_ref, ht_ref, hot_ref = refs[:5]
    refs = refs[5:]
    if earlier:
        refs = refs[1:]
    done = ()
    if merge:
        done, refs = refs[: 2 * earlier], refs[2 * earlier :]
    down_ref, pre_ref, gate_ref = refs[:3]
    dz_ref = refs[3]

    @pl.when(pl.program_id(0) == 0)
    def _():
        size = shards[0].shape[0]
        for k in range(parts):
            start = pl.multiple_of(idx_ref[k] * size, 16)
            dz_ref[pl.ds(start, size), :] = shards[k][...]

    dz = dz_ref[...]
    d_hidden = lax.dot_general(
        dz, w_ref[0], (((1,), (1,)), ((), ())), preferred_element_type=F32
    )
    down_ref[0] = jnp.dot(ht_ref[0], dz, preferred_element_type=F32).astype(BF16)
    product = d_hidden * act_ref[0]
    high = product.astype(BF16)
    low = (product - high.astype(F32)).astype(BF16)
    hot = hot_ref[...]
    d_gate = jnp.dot(hot, high, preferred_element_type=F32) + jnp.dot(
        hot, low, preferred_element_type=F32
    )
    d_pre = d_hidden * mul_ref[0]
    if not merge:
        pre_ref[...] = d_pre.astype(BF16)
        gate_ref[...] = d_gate
    else:
        rows_ref = refs[4]
        count, toks, block = pre_ref.shape
        for t in range(earlier):
            put_rows(rows_ref, t, count, toks, done[2 * t][...].astype(F32))
            gate_ref[:, t, :] = done[2 * t + 1][...]
        put_rows(rows_ref, earlier, count, toks, d_pre)
        gate_ref[:, earlier, :] = d_gate
        spill(rows_ref, pre_ref)


def token_step(t, idx, shards, down_weight, act, mul, ht, hot_t, down, done, block):
    toks, hidden, width = down_weight.shape
    count = act.shape[1]
    scen = hot_t.shape[0]
    parts = len(shards)
    size = shards[0].shape[0]
    merge = t == toks - 1
    operands = list(shards) + [down_weight, act, mul, ht, hot_t]
    specs = [pl.BlockSpec((size, width), lambda i, s: (0, 0))] * parts + [
        pl.BlockSpec((1, block, width), lambda i, s: (t, i, 0)),
        pl.BlockSpec((1, count, block), lambda i, s: (t, 0, i)),
        pl.BlockSpec((1, count, block), lambda i, s: (t, 0, i)),
        pl.BlockSpec((1, block, count), lambda i, s: (t, i, 0)),
        pl.BlockSpec((scen, count), lambda i, s: (0, 0)),
    ]
    aliases = {}
    if t:
        aliases = {1 + len(operands): 0}
        operands.append(down)
        specs.append(pl.BlockSpec(memory_space=pl.ANY))
    scratch = [pltpu.VMEM((count, width), BF16)]
    if merge:
        for pre, gate in done:
            operands += [pre, gate]
            specs += [
                pl.BlockSpec((count, block), lambda i, s: (0, i)),
                pl.BlockSpec((scen, block), lambda i, s: (0, i)),
            ]
        scratch.append(pltpu.VMEM((block // 128, count * toks, 128), F32))
        pre_spec = pl.BlockSpec((count, toks, block), lambda i, s: (0, 0, i))
        gate_spec = pl.BlockSpec((scen, toks, block), lambda i, s: (0, 0, i))
        pre_shape, gate_shape = (count, toks, hidden), (scen, toks, hidden)
    else:
        pre_spec = pl.BlockSpec((count, block), lambda i, s: (0, i))
        gate_spec = pl.BlockSpec((scen, block), lambda i, s: (0, i))
        pre_shape, gate_shape = (count, hidden), (scen, hidden)
    return pl.pallas_call(
        functools.partial(token_kernel, parts, t, merge),
        grid_spec=pltpu.PrefetchScalarGridSpec(
            num_scalar_prefetch=1,
            grid=(hidden // block,),
            in_specs=specs,
            out_specs=[pl.BlockSpec((1, block, width), lambda i, s: (t, i, 0)), pre_spec, gate_spec],
            scratch_shapes=scratch,
        ),
        out_shape=(
            jax.ShapeDtypeStruct(down_weight.shape, BF16),
            jax.ShapeDtypeStruct(pre_shape, BF16),
            jax.ShapeDtypeStruct(gate_shape, F32),
        ),
        input_output_aliases=aliases,
        compiler_params=pltpu.CompilerParams(vmem_limit_bytes=24 * MIB),
        cost_estimate=pl.CostEstimate(
            flops=4 * count * hidden * width,
            bytes_accessed=4 * hidden * width + 12 * count * hidden,
            transcendentals=0,
        ),
        name="token",
    )(idx, *operands)


def plain_tokens(dz, pre_act, gates, down_weight, scenario):
    piece = lax.all_gather(dz, "dp", axis=1, tiled=True)
    onehot = (scenario[:, None] == jnp.arange(gates.shape[0], dtype=jnp.int32)[None, :]).astype(F32)
    rate = jnp.einsum("bs,stf->btf", onehot, gates, precision=lax.Precision.HIGHEST)
    activated, slope = gelu_parts(pre_act.astype(F32))
    hidden = (activated * rate).astype(BF16)
    d_hidden = jnp.einsum("tbc,tfc->btf", piece, down_weight, preferred_element_type=F32)
    gate = jnp.einsum("bs,btf->stf", onehot, d_hidden * activated, precision=lax.Precision.HIGHEST)
    pre = (d_hidden * rate * slope).astype(BF16)
    down = jnp.einsum("btf,tbc->tfc", hidden, piece, preferred_element_type=F32).astype(BF16)
    return pre, down, gate


def ring_tokens(dz, pre_act, gates, down_weight, scenario):
    dp = lax.axis_size("dp")
    toks = dz.shape[0]
    order = ring_order(dp)
    ring = [(order[k], order[(k + 1) % dp]) for k in range(dp)]
    sources = np.zeros((dp, dp), np.int32)
    for k in range(dp):
        for s in range(dp):
            sources[order[k], s] = order[(k - s) % dp]
    idx = lax.dynamic_index_in_dim(jnp.asarray(sources), lax.axis_index("dp"), 0, keepdims=False)

    shards = [[dz[t]] for t in range(toks)]
    for s in range(dp - 1):
        for t in range(toks):
            shards[t].append(lax.ppermute(shards[t][-1], "dp", ring))

    count = gates.shape[0]
    hot = (scenario[:, None] == jnp.arange(count, dtype=jnp.int32)[None, :]).astype(BF16)
    hot_t = (jnp.arange(count, dtype=jnp.int32)[:, None] == scenario[None, :]).astype(BF16)
    block = 256
    ht, act, mul = activations(pre_act, gates, hot, block)

    down, done = None, []
    for t in range(toks):
        down, pre, gate = token_step(
            t, idx, shards[t], down_weight, act, mul, ht, hot_t, down, done, block
        )
        done.append((pre, gate))
    return pre, down, gate


def per_device(pre_norm, cotangent, gain, pre_act, gates, down_weight, scenario):
    dp = lax.axis_size("dp")
    groups = lax.axis_size("tok")
    toks = pre_norm.shape[1]
    dz, send, gain_parts = norm(pre_norm, cotangent, gain, dp, groups)
    recv = lax.all_to_all(send, "tok", 0, 0, tiled=True)
    d_input = mix(recv, dz)
    gain_gradient = jnp.sum(lax.all_to_all(gain_parts, "dp", 0, 0, tiled=True), axis=0)

    if down_weight.shape[1] % 256:
        pre, down, gate = plain_tokens(dz, pre_act, gates, down_weight, scenario)
    else:
        pre, down, gate = ring_tokens(dz, pre_act, gates, down_weight, scenario)
    return (d_input, pre, down, gate, gain_gradient)


def solution(mesh):
    placed = (
        P(("group", "dp"), "tok", None),
        P(("group", "dp"), "tok", None),
        P("tok", None),
        P("group", "tok", "dp"),
        P(None, "tok", "dp"),
        P("tok", "dp", None),
        P("group"),
    )
    return jax.shard_map(
        per_device,
        mesh=mesh,
        in_specs=placed,
        out_specs=(
            P(("group", "dp"), "tok", None),
            P("group", "tok", "dp"),
            P(("group", "tok"), "dp", None),
            P("group", "tok", "dp"),
            P(("group", "tok"), "dp"),
        ),
        check_vma=False,
    )
```

```python
import functools
import jax
import jax.numpy as jnp
from jax import lax
from jax.experimental import pallas as pl
from jax.experimental.pallas import tpu as pltpu
from jax.sharding import PartitionSpec as P

F32 = jnp.float32
BF16 = jnp.bfloat16
LIMIT = 56 << 20


def gelu_parts(value):
    square = value * value
    tangent = jnp.tanh(value * (0.7978845608 + (0.7978845608 * 0.044715) * square))
    half = 0.5 + 0.5 * tangent
    activated = value * half
    slope = half + activated * (1.0 - tangent) * (
        0.7978845608 + (0.7978845608 * 3.0 * 0.044715) * square
    )
    return activated, slope


def pin(value):
    return pltpu.with_memory_space_constraint(value, pltpu.HBM)


def ring_order(count):
    return [0] + list(range(1, count, 2)) + list(range(2, count, 2))[::-1]


def take_rows(rows_ref, t, count, toks):
    return jnp.concatenate(
        [rows_ref[j, pl.ds(t, count, stride=toks), :] for j in range(rows_ref.shape[0])], axis=1
    )


def put_rows(rows_ref, t, count, toks, value, first=0):
    for j in range(value.shape[1] // 128):
        rows_ref[first + j, pl.ds(t, count, stride=toks), :] = value[:, j * 128 : (j + 1) * 128]


def spill(rows_ref, out_ref):
    count, toks, width = out_ref.shape
    for j in range(width // 128):
        out_ref[:, :, j * 128 : (j + 1) * 128] = (
            rows_ref[j].reshape(count, toks, 128).astype(out_ref.dtype)
        )


def norm_kernel(pieces, chunks, x_hbm, g_hbm, gain_hbm, *refs):
    dz_refs, refs = refs[:chunks], refs[chunks:]
    send_refs, (gg_ref, x_ref, g_ref, gain_ref, rows_ref, sems) = refs[:-6], refs[-6:]
    count, toks, width = x_ref.shape
    gain_copy = pltpu.make_async_copy(gain_hbm, gain_ref, sems.at[2 * pieces])
    gain_copy.start()
    size = count // pieces
    copies = []
    for k in range(pieces):
        part = pl.ds(k * size, size)
        pair = (
            pltpu.make_async_copy(x_hbm.at[part], x_ref.at[part], sems.at[2 * k]),
            pltpu.make_async_copy(g_hbm.at[part], g_ref.at[part], sems.at[2 * k + 1]),
        )
        for copy in pair:
            copy.start()
        copies.append(pair)
    gain_copy.wait()
    step = 8 // toks
    gain = jnp.concatenate([gain_ref[...]] * step, axis=0)
    scale = 1.0 / width
    total = jnp.zeros((8, width), F32)
    for i in range(count // step):
        if i * step % size == 0:
            for copy in copies[i * step // size]:
                copy.wait()
        x = x_ref[i * step : (i + 1) * step].astype(F32).reshape(8, width)
        ct = g_ref[i * step : (i + 1) * step].astype(F32).reshape(8, width)
        g = ct * gain
        c = x - jnp.sum(x, axis=-1, keepdims=True) * scale
        mean_g = jnp.sum(g, axis=-1, keepdims=True) * scale
        rstd = lax.rsqrt(jnp.sum(c * c, axis=-1, keepdims=True) * scale + 1e-05)
        mean_gc = jnp.sum(g * c, axis=-1, keepdims=True) * scale
        xhat = c * rstd
        total = total + ct * xhat
        dz = rstd * (g - mean_g - xhat * (mean_gc * rstd))
        for j in range(width // 128):
            rows_ref[j, i * 8 : (i + 1) * 8, :] = dz[:, j * 128 : (j + 1) * 128]
    part = sum(total[k * toks : (k + 1) * toks] for k in range(step))
    gg_ref[...] = part
    dz = [ref.at[i] for ref in dz_refs for i in range(ref.shape[0])]
    for t in range(toks):
        dz[t][:, :width] = take_rows(rows_ref, t, count, toks).astype(BF16)
    if dz[0].shape[1] > width:
        high = part.astype(BF16).astype(F32)
        for k, value in enumerate((high, part - high)):
            lines = [
                value[i : i + 1, j : j + 128] for i in range(toks) for j in range(0, width, 128)
            ]
            dz[0][:, width + 128 * k : width + 128 * (k + 1)] = jnp.concatenate(
                lines, axis=0
            ).astype(BF16)
    me = lax.axis_index("tok")
    block = width // (1 + len(send_refs))
    for k, send_ref in enumerate(send_refs):
        start = pl.multiple_of((me ^ (k + 1)) * block, 128)
        for t in range(toks):
            send_ref[t] = dz[t][:, pl.ds(start, block)]


def norm(pre_norm, cotangent, gain, groups, chunks, spare):
    count, toks, width = pre_norm.shape
    pieces = 4
    return pl.pallas_call(
        functools.partial(norm_kernel, pieces, len(chunks)),
        out_shape=[
            jax.ShapeDtypeStruct((size, count, width + (0 if i else spare)), BF16)
            for i, size in enumerate(chunks)
        ]
        + [jax.ShapeDtypeStruct((toks, count, width // groups), BF16)] * (groups - 1)
        + [jax.ShapeDtypeStruct((toks, width), F32)],
        in_specs=[pl.BlockSpec(memory_space=pltpu.HBM)] * 3,
        out_specs=[pl.BlockSpec(memory_space=pltpu.VMEM)] * (len(chunks) + groups),
        scratch_shapes=[
            pltpu.VMEM((count, toks, width), BF16),
            pltpu.VMEM((count, toks, width), BF16),
            pltpu.VMEM((toks, width), F32),
            pltpu.VMEM((width // 128, count * toks, 128), F32),
            pltpu.SemaphoreType.DMA((2 * pieces + 1,)),
        ],
        compiler_params=pltpu.CompilerParams(vmem_limit_bytes=12 << 20),
        name="norm",
    )(pin(pre_norm), pin(cotangent), pin(gain))


def mix_kernel(groups, *refs):
    recv_refs, dz_refs, (out_ref, rows_ref) = refs[: groups - 1], refs[groups - 1 : -2], refs[-2:]
    dz_refs = [ref.at[i] for ref in dz_refs for i in range(ref.shape[0])]
    count, toks, width = out_ref.shape
    block = width // (1 + len(recv_refs))
    piece = block // toks
    me = lax.axis_index("tok")
    for k in range(1 + len(recv_refs)):
        start = pl.multiple_of((me ^ k) * block, 128)
        if k:
            got = [recv_refs[k - 1][i].astype(F32) for i in range(toks)]
        else:
            got = [dz_refs[i][:, pl.ds(start, block)].astype(F32) for i in range(toks)]
        for j in range(toks):
            mixed = jnp.concatenate(
                [got[i][:, j * piece : (j + 1) * piece] for i in range(toks)], axis=1
            )
            mixed = mixed + dz_refs[j][:, pl.ds(start, block)].astype(F32)
            put_rows(rows_ref, j, count, toks, mixed, (me ^ k) * (block // 128))
    spill(rows_ref, out_ref)


def mix(recv, dz, width):
    toks = sum(v.shape[0] for v in dz)
    count = dz[0].shape[1]
    return pl.pallas_call(
        functools.partial(mix_kernel, 1 + len(recv)),
        out_shape=jax.ShapeDtypeStruct((count, toks, width), BF16),
        in_specs=[pl.BlockSpec(memory_space=pltpu.VMEM)] * (len(recv) + len(dz)),
        out_specs=pl.BlockSpec(memory_space=pltpu.VMEM),
        scratch_shapes=[pltpu.VMEM((width // 128, count * toks, 128), F32)],
        compiler_params=pltpu.CompilerParams(vmem_limit_bytes=8 << 20),
        cost_estimate=pl.CostEstimate(flops=1, bytes_accessed=1, transcendentals=0),
        name="mix",
    )(*recv, *dz)


def one_hot(scenario_ref, count):
    return (
        lax.broadcasted_iota(jnp.int32, (count, scenario_ref.shape[1]), 0) == scenario_ref[...]
    ).astype(BF16)


def act_kernel(parts, first, toks, source, gates_hbm, pick, w_hbm, *refs):
    h_ref, act_ref, mul_ref, w_ref, refs = *refs[:4], refs[4:]
    count, width = act_ref.shape[1:]
    held = act_ref.shape[0]
    block = width // parts
    cols = block // 128
    if not first:
        hot_ref, rest_ref, pre_ref, scenario_ref, rows_ref, *refs = refs
    gates_ref, sems = refs
    copies = [pltpu.make_async_copy(gates_hbm, gates_ref, sems.at[0])]
    if not first:
        copies.append(pltpu.make_async_copy(pick, scenario_ref, sems.at[1]))
        for i in range(parts):
            part = pl.ds(i * block, block)
            copies.append(
                pltpu.make_async_copy(source.at[:, :, part], pre_ref.at[:, :, part], sems.at[2 + i])
            )
    weights = [
        pltpu.make_async_copy(w_hbm.at[first + t], w_ref.at[t], sems.at[2 + parts + t])
        for t in range(held)
    ]
    for copy in copies + weights:
        copy.start()
    copies[0].wait()
    if first:
        hot = pick[...]
    else:
        copies[1].wait()
        hot = one_hot(scenario_ref, gates_ref.shape[0])
        hot_ref[...] = hot
    hot = jnp.concatenate([hot] * 3, axis=0)
    for i in range(parts):
        part = slice(i * block, (i + 1) * block)
        if not first:
            copies[2 + i].wait()
            for j in range(cols):
                lane = i * block + j * 128
                rows_ref[j] = (
                    pre_ref[:, :, lane : lane + 128].astype(F32).reshape(count * toks, 128)
                )
            for t in range(held, toks):
                rest_ref[t - held, :, part] = take_rows(rows_ref, t, count, toks)
        for t in range(held):
            gate = gates_ref[:, first + t, part]
            high = gate.astype(BF16)
            rest = gate - high.astype(F32)
            mid = rest.astype(BF16)
            low = (rest - mid.astype(F32)).astype(BF16)
            rate = lax.dot_general(
                hot,
                jnp.concatenate([high, mid, low], axis=0),
                (((0,), (0,)), ((), ())),
                preferred_element_type=F32,
            )
            value = source[t, :, part] if first else take_rows(rows_ref, t, count, toks)
            activated, slope = gelu_parts(value)
            h_ref[t, :, part] = (activated * rate).astype(BF16)
            act_ref[t, :, part] = activated
            mul_ref[t, :, part] = rate * slope
    for copy in weights:
        copy.wait()


def activations(first, source, gates, pick, down_weight):
    scen, toks, width = gates.shape
    count = source.shape[1] if first else source.shape[0]
    held = toks // 2
    parts = width // 512
    vmem = pl.BlockSpec(memory_space=pltpu.VMEM)
    hbm = pl.BlockSpec(memory_space=pltpu.HBM)
    shapes = [
        jax.ShapeDtypeStruct((held, count, width), BF16),
        jax.ShapeDtypeStruct((held, count, width), F32),
        jax.ShapeDtypeStruct((held, count, width), F32),
        jax.ShapeDtypeStruct((held,) + down_weight.shape[1:], BF16),
    ]
    scratch = [pltpu.VMEM(gates.shape, F32), pltpu.SemaphoreType.DMA((2 + parts + held,))]
    if not first:
        shapes += [
            jax.ShapeDtypeStruct((scen, count), BF16),
            jax.ShapeDtypeStruct((toks - held, count, width), F32),
        ]
        scratch = [
            pltpu.VMEM((count, toks, width), BF16),
            pltpu.VMEM(pick.shape, jnp.int32),
            pltpu.VMEM((512 // 128, count * toks, 128), F32),
        ] + scratch
        source, pick = pin(source), pin(pick)
    return pl.pallas_call(
        functools.partial(act_kernel, parts, first, toks),
        in_specs=[vmem, hbm, vmem, hbm] if first else [hbm] * 4,
        out_specs=[vmem] * len(shapes),
        out_shape=shapes,
        scratch_shapes=scratch,
        compiler_params=pltpu.CompilerParams(vmem_limit_bytes=14 << 20),
        cost_estimate=pl.CostEstimate(flops=1, bytes_accessed=1, transcendentals=0),
        name="act",
    )(source, pin(gates), pick, pin(down_weight))


def token_kernel(t, at, parts, merge, sources, *refs):
    chunks, refs = refs[:parts], refs[parts:]
    shards = [chunk.at[at] for chunk in chunks]
    all_w, all_act, all_mul, all_h, hot_ref = refs[:5]
    w_ref, act_ref, mul_ref, h_ref = [ref.at[t % 2] for ref in (all_w, all_act, all_mul, all_h)]
    refs = refs[5:]
    if t:
        refs = refs[1:]
    done = ()
    if merge:
        done, refs = refs[: 2 * t], refs[2 * t :]
    down_hbm, pre_ref, gate_ref = refs[:3]
    refs = refs[3:]
    if not t:
        gain_ref, refs = refs[0], refs[1:]
    dz_ref, out_ref, sems = refs[:3]

    me = lax.axis_index("dp")
    size = shards[0].shape[0]
    width = dz_ref.shape[1]
    for k in range(parts):
        place = sum(jnp.where(me == m, sources[m][k], 0) for m in range(parts))
        start = pl.multiple_of(place * size, 16)
        dz_ref[pl.ds(start, size), :] = shards[k][:, :width]
    if not t:
        total = sum(shard[:, width + i : width + i + 128].astype(F32) for shard in shards for i in (0, 128))
        lines_ref = refs[3]
        lines_ref[...] = total
        share = gain_ref.shape[1] // 128
        cols = width // 128
        for i in range(gain_ref.shape[0]):
            for j in range(share):
                gain_ref[i : i + 1, j * 128 : (j + 1) * 128] = lines_ref[
                    pl.ds(i * cols + me * share + j, 1), :
                ]
    dz = dz_ref[...]
    hidden = out_ref.shape[0]
    block = hidden // 3
    hot = hot_ref[...]
    writes = []

    def write(source, target, k):
        writes.append(pltpu.make_async_copy(source, target, sems.at[k]))
        writes[-1].start()

    def down(i):
        rows = pl.ds(i * block, block)
        out_ref[i * block : (i + 1) * block] = lax.dot_general(
            h_ref[:, i * block : (i + 1) * block],
            dz,
            (((0,), (0,)), ((), ())),
            preferred_element_type=F32,
        ).astype(BF16)
        write(out_ref.at[rows], down_hbm.at[t, rows], i)

    def back(i):
        part = slice(i * block, (i + 1) * block)
        d_hidden = lax.dot_general(
            dz, w_ref[part], (((1,), (1,)), ((), ())), preferred_element_type=F32
        )
        product = d_hidden * act_ref[:, part]
        high = product.astype(BF16)
        low = (product - high.astype(F32)).astype(BF16)
        d_gate = jnp.dot(hot, high, preferred_element_type=F32) + jnp.dot(
            hot, low, preferred_element_type=F32
        )
        d_pre = d_hidden * mul_ref[:, part]
        if not merge:
            pre_ref[:, part] = d_pre.astype(BF16)
            gate_ref[:, part] = d_gate
            return
        rows_ref, spill_ref = refs[3:5]
        count, toks, _ = pre_ref.shape
        for k in range(t):
            put_rows(rows_ref, k, count, toks, done[2 * k][:, part].astype(F32))
            gate_ref[:, k, part] = done[2 * k + 1][:, part]
        put_rows(rows_ref, t, count, toks, d_pre)
        gate_ref[:, t, part] = d_gate
        if i > 1:
            writes[2 * i - 3].wait()
        spill(rows_ref, spill_ref.at[i % 2])
        write(spill_ref.at[i % 2], pre_ref.at[:, :, pl.ds(i * block, block)], 3 + i)

    for i in range(3):
        down(i)
        back(i)
    for k, copy in enumerate(writes):
        if not merge or k != 1:
            copy.wait()


def token_step(t, at, toks, sources, shards, held, act, mul, h, hot, down, done):
    hidden, width = held.shape[1:]
    scen, count = hot.shape
    parts = len(shards)
    merge = t == toks - 1
    anywhere = pl.BlockSpec(memory_space=pltpu.HBM)
    vmem = pl.BlockSpec(memory_space=pltpu.VMEM)
    operands = list(shards) + [held, act, mul, h, hot]
    specs = [vmem] * (parts + 5)
    aliases = {}
    if t:
        aliases = {len(operands): 0}
        operands.append(down)
        specs.append(anywhere)
    scratch = [
        pltpu.VMEM((count, width), BF16),
        pltpu.VMEM((hidden, width), BF16),
        pltpu.SemaphoreType.DMA((6,)),
    ]
    if merge:
        for pre, gate in done:
            operands += [pre, gate]
            specs += [vmem, vmem]
        scratch.append(pltpu.VMEM((hidden // 3 // 128, count * toks, 128), F32))
        scratch.append(pltpu.VMEM((2, count, toks, hidden // 3), BF16))
        pre_shape, gate_shape = (count, toks, hidden), (scen, toks, hidden)
    else:
        pre_shape, gate_shape = (count, hidden), (scen, hidden)
    shapes = [
        jax.ShapeDtypeStruct((toks, hidden, width), BF16),
        jax.ShapeDtypeStruct(pre_shape, BF16),
        jax.ShapeDtypeStruct(gate_shape, F32),
    ]
    if not t:
        shapes.append(jax.ShapeDtypeStruct((toks, width // parts), F32))
        scratch.append(pltpu.VMEM((shards[0].shape[1], 128), F32))
    return pl.pallas_call(
        functools.partial(token_kernel, t, at, parts, merge, sources),
        in_specs=specs,
        out_specs=[anywhere, anywhere if merge else vmem] + [vmem] * (len(shapes) - 2),
        scratch_shapes=scratch,
        out_shape=shapes,
        input_output_aliases=aliases,
        compiler_params=pltpu.CompilerParams(vmem_limit_bytes=14 << 20),
        cost_estimate=pl.CostEstimate(flops=1, bytes_accessed=1, transcendentals=0),
        name="token",
    )(*operands)


def plain_tokens(dz, pre_act, gates, down_weight, scenario):
    piece = lax.all_gather(dz, "dp", axis=1, tiled=True)
    onehot = (scenario[:, None] == jnp.arange(gates.shape[0], dtype=jnp.int32)[None, :]).astype(F32)
    rate = jnp.einsum("bs,stf->btf", onehot, gates, precision=lax.Precision.HIGHEST)
    activated, slope = gelu_parts(pre_act.astype(F32))
    hidden = (activated * rate).astype(BF16)
    d_hidden = jnp.einsum("tbc,tfc->btf", piece, down_weight, preferred_element_type=F32)
    gate = jnp.einsum("bs,btf->stf", onehot, d_hidden * activated, precision=lax.Precision.HIGHEST)
    pre = (d_hidden * rate * slope).astype(BF16)
    down = jnp.einsum("btf,tbc->tfc", hidden, piece, preferred_element_type=F32).astype(BF16)
    return pre, down, gate


def after(value, *others):
    return lax.optimization_barrier((value, *others))[0]


def swap(send):
    groups = 1 + len(send)
    return [
        lax.ppermute(v, "tok", [(p, p ^ (k + 1)) for p in range(groups)]) for k, v in enumerate(send)
    ]


def ring_tokens(dz, send, pre_act, gates, down_weight, scenario):
    dp = lax.axis_size("dp")
    order = ring_order(dp)
    ring = [(order[k], order[(k + 1) % dp]) for k in range(dp)]
    place = {device: k for k, device in enumerate(order)}
    sources = [[order[(place[m] - s) % dp] for s in range(dp)] for m in range(dp)]
    shards = [[v] for v in dz]

    def hop(i, *others):
        last = shards[i][-1]
        shards[i].append(lax.ppermute(after(last, *others) if others else last, "dp", ring))

    for i in range(4):
        hop(i)
    recv = swap(send)
    h, act, mul, held, hot, rest = [
        [v] for v in activations(0, pre_act, gates, scenario.reshape(1, -1), down_weight)
    ]
    hop(0, h[0])
    hop(1, h[0])
    hot, rest = hot[0], rest[0]
    more = activations(2, rest, gates, hot, down_weight)
    for have, new in zip((h, act, mul, held), more):
        have.append(new)
    d_input = mix([after(r, h[0]) for r in recv], dz, down_weight.shape[2])
    hop(2)
    hop(3)
    hop(0)
    hop(1, h[1])
    hot = after(hot, d_input)

    down, done = None, []
    homes = [(i, k) for i, v in enumerate(dz) for k in range(v.shape[0])]
    for t, (i, at) in enumerate(homes):
        down, pre, gate, *more = token_step(
            t, at, len(homes), sources, shards[i], held[t // 2], act[t // 2], mul[t // 2], h[t // 2], hot, down, done
        )
        done.append((pre, gate))
        if t == 0:
            gain_gradient = more[0]
            hop(2, gate)
        if t == 1:
            hop(3, gate)
    return d_input, pre, down, gate, gain_gradient


def per_device(pre_norm, cotangent, gain, pre_act, gates, down_weight, scenario):
    groups = lax.axis_size("tok")
    toks, width = gain.shape
    fits = down_weight.shape[1] == 1536 and toks == 4 and lax.axis_size("dp") == 4
    chunks, spare = ((1, 1, 1, 1), 256) if fits else ((toks,), 0)
    outs = norm(pre_norm, cotangent, gain, groups, chunks, spare)
    dz, send, gain_part = outs[: len(chunks)], outs[len(chunks) : -1], outs[-1]
    if fits:
        return ring_tokens(dz, send, pre_act, gates, down_weight, scenario)
    d_input = mix(swap(send), dz, width)
    pre, down, gate = plain_tokens(dz[0], pre_act, gates, down_weight, scenario)
    gain_gradient = lax.psum_scatter(gain_part, "dp", scatter_dimension=1, tiled=True)
    return d_input, pre, down, gate, gain_gradient


def solution(mesh):
    placed = (
        P(("group", "dp"), "tok", None),
        P(("group", "dp"), "tok", None),
        P("tok", None),
        P("group", "tok", "dp"),
        P(None, "tok", "dp"),
        P("tok", "dp", None),
        P("group"),
    )
    return jax.shard_map(
        per_device,
        mesh=mesh,
        in_specs=placed,
        out_specs=(
            P(("group", "dp"), "tok", None),
            P("group", "tok", "dp"),
            P(("group", "tok"), "dp", None),
            P("group", "tok", "dp"),
            P(("group", "tok"), "dp"),
        ),
        check_vma=False,
    )
```

```python
import functools
import jax
import jax.numpy as jnp
from jax import lax
from jax.experimental import pallas as pl
from jax.experimental.pallas import tpu as pltpu
from jax.sharding import PartitionSpec as P

F32 = jnp.float32
BF16 = jnp.bfloat16
LIMIT = 56 << 20


def gelu_parts(value):
    square = value * value
    tangent = jnp.tanh(value * (0.7978845608 + (0.7978845608 * 0.044715) * square))
    half = 0.5 + 0.5 * tangent
    activated = value * half
    slope = half + activated * (1.0 - tangent) * (
        0.7978845608 + (0.7978845608 * 3.0 * 0.044715) * square
    )
    return activated, slope


def pin(value):
    return pltpu.with_memory_space_constraint(value, pltpu.HBM)


def ring_order(count):
    return [0] + list(range(1, count, 2)) + list(range(2, count, 2))[::-1]


def take_rows(rows_ref, t, count, toks):
    return jnp.concatenate(
        [rows_ref[j, pl.ds(t, count, stride=toks), :] for j in range(rows_ref.shape[0])], axis=1
    )


def put_rows(rows_ref, t, count, toks, value, first=0):
    for j in range(value.shape[1] // 128):
        rows_ref[first + j, pl.ds(t, count, stride=toks), :] = value[:, j * 128 : (j + 1) * 128]


def spill(rows_ref, out_ref):
    count, toks, width = out_ref.shape
    for j in range(width // 128):
        out_ref[:, :, j * 128 : (j + 1) * 128] = (
            rows_ref[j].reshape(count, toks, 128).astype(out_ref.dtype)
        )


def norm_kernel(pieces, chunks, x_hbm, g_hbm, gain_hbm, *refs):
    dz_refs, refs = refs[:chunks], refs[chunks:]
    send_refs, (gg_ref, x_ref, g_ref, gain_ref, rows_ref, sems) = refs[:-6], refs[-6:]
    count, toks, width = x_ref.shape
    gain_copy = pltpu.make_async_copy(gain_hbm, gain_ref, sems.at[2 * pieces])
    gain_copy.start()
    size = count // pieces
    copies = []
    for k in range(pieces):
        part = pl.ds(k * size, size)
        pair = (
            pltpu.make_async_copy(x_hbm.at[part], x_ref.at[part], sems.at[2 * k]),
            pltpu.make_async_copy(g_hbm.at[part], g_ref.at[part], sems.at[2 * k + 1]),
        )
        for copy in pair:
            copy.start()
        copies.append(pair)
    gain_copy.wait()
    step = 8 // toks
    gain = jnp.concatenate([gain_ref[...]] * step, axis=0)
    scale = 1.0 / width
    total = jnp.zeros((8, width), F32)
    for i in range(count // step):
        if i * step % size == 0:
            for copy in copies[i * step // size]:
                copy.wait()
        x = x_ref[i * step : (i + 1) * step].astype(F32).reshape(8, width)
        ct = g_ref[i * step : (i + 1) * step].astype(F32).reshape(8, width)
        g = ct * gain
        c = x - jnp.sum(x, axis=-1, keepdims=True) * scale
        mean_g = jnp.sum(g, axis=-1, keepdims=True) * scale
        rstd = lax.rsqrt(jnp.sum(c * c, axis=-1, keepdims=True) * scale + 1e-05)
        mean_gc = jnp.sum(g * c, axis=-1, keepdims=True) * scale
        xhat = c * rstd
        total = total + ct * xhat
        dz = rstd * (g - mean_g - xhat * (mean_gc * rstd))
        for j in range(width // 128):
            rows_ref[j, i * 8 : (i + 1) * 8, :] = dz[:, j * 128 : (j + 1) * 128]
    part = sum(total[k * toks : (k + 1) * toks] for k in range(step))
    gg_ref[...] = part
    dz = [ref.at[i] for ref in dz_refs for i in range(ref.shape[0])]
    for t in range(toks):
        dz[t][:, :width] = take_rows(rows_ref, t, count, toks).astype(BF16)
    if dz[0].shape[1] > width:
        high = part.astype(BF16).astype(F32)
        for k, value in enumerate((high, part - high)):
            lines = [
                value[i : i + 1, j : j + 128] for i in range(toks) for j in range(0, width, 128)
            ]
            dz[0][:, width + 128 * k : width + 128 * (k + 1)] = jnp.concatenate(
                lines, axis=0
            ).astype(BF16)
    me = lax.axis_index("tok")
    block = width // (1 + len(send_refs))
    for k, send_ref in enumerate(send_refs):
        start = pl.multiple_of((me ^ (k + 1)) * block, 128)
        for t in range(toks):
            send_ref[t] = dz[t][:, pl.ds(start, block)]


def norm(pre_norm, cotangent, gain, groups, chunks, spare):
    count, toks, width = pre_norm.shape
    pieces = 4
    return pl.pallas_call(
        functools.partial(norm_kernel, pieces, len(chunks)),
        out_shape=[
            jax.ShapeDtypeStruct((size, count, width + (0 if i else spare)), BF16)
            for i, size in enumerate(chunks)
        ]
        + [jax.ShapeDtypeStruct((toks, count, width // groups), BF16)] * (groups - 1)
        + [jax.ShapeDtypeStruct((toks, width), F32)],
        in_specs=[pl.BlockSpec(memory_space=pltpu.HBM)] * 3,
        out_specs=[pl.BlockSpec(memory_space=pltpu.VMEM)] * (len(chunks) + groups),
        scratch_shapes=[
            pltpu.VMEM((count, toks, width), BF16),
            pltpu.VMEM((count, toks, width), BF16),
            pltpu.VMEM((toks, width), F32),
            pltpu.VMEM((width // 128, count * toks, 128), F32),
            pltpu.SemaphoreType.DMA((2 * pieces + 1,)),
        ],
        compiler_params=pltpu.CompilerParams(vmem_limit_bytes=12 << 20),
        name="norm",
    )(pin(pre_norm), pin(cotangent), pin(gain))


def mix_kernel(groups, *refs):
    recv_refs, dz_refs, (out_ref, rows_ref) = refs[: groups - 1], refs[groups - 1 : -2], refs[-2:]
    dz_refs = [ref.at[i] for ref in dz_refs for i in range(ref.shape[0])]
    count, toks, width = out_ref.shape
    block = width // (1 + len(recv_refs))
    piece = block // toks
    me = lax.axis_index("tok")
    for k in range(1 + len(recv_refs)):
        start = pl.multiple_of((me ^ k) * block, 128)
        if k:
            got = [recv_refs[k - 1][i].astype(F32) for i in range(toks)]
        else:
            got = [dz_refs[i][:, pl.ds(start, block)].astype(F32) for i in range(toks)]
        for j in range(toks):
            mixed = jnp.concatenate(
                [got[i][:, j * piece : (j + 1) * piece] for i in range(toks)], axis=1
            )
            mixed = mixed + dz_refs[j][:, pl.ds(start, block)].astype(F32)
            put_rows(rows_ref, j, count, toks, mixed, (me ^ k) * (block // 128))
    spill(rows_ref, out_ref)


def mix(recv, dz, width):
    toks = sum(v.shape[0] for v in dz)
    count = dz[0].shape[1]
    return pl.pallas_call(
        functools.partial(mix_kernel, 1 + len(recv)),
        out_shape=jax.ShapeDtypeStruct((count, toks, width), BF16),
        in_specs=[pl.BlockSpec(memory_space=pltpu.VMEM)] * (len(recv) + len(dz)),
        out_specs=pl.BlockSpec(memory_space=pltpu.VMEM),
        scratch_shapes=[pltpu.VMEM((width // 128, count * toks, 128), F32)],
        compiler_params=pltpu.CompilerParams(vmem_limit_bytes=8 << 20),
        cost_estimate=pl.CostEstimate(flops=1, bytes_accessed=1, transcendentals=0),
        name="mix",
    )(*recv, *dz)


def one_hot(scenario_ref, count):
    return (
        lax.broadcasted_iota(jnp.int32, (count, scenario_ref.shape[1]), 0) == scenario_ref[...]
    ).astype(BF16)


def act_kernel(parts, first, toks, source, gates_hbm, pick, w_hbm, *refs):
    h_ref, act_ref, mul_ref, w_ref, refs = *refs[:4], refs[4:]
    count, width = act_ref.shape[1:]
    held = act_ref.shape[0]
    block = width // parts
    cols = block // 128
    if not first:
        hot_ref, rest_ref, pre_ref, scenario_ref, rows_ref, *refs = refs
    gates_ref, sems = refs
    copies = [pltpu.make_async_copy(gates_hbm, gates_ref, sems.at[0])]
    if not first:
        copies.append(pltpu.make_async_copy(pick, scenario_ref, sems.at[1]))
        for i in range(parts):
            part = pl.ds(i * block, block)
            copies.append(
                pltpu.make_async_copy(source.at[:, :, part], pre_ref.at[:, :, part], sems.at[2 + i])
            )
    weights = [
        pltpu.make_async_copy(w_hbm.at[first + t], w_ref.at[t], sems.at[2 + parts + t])
        for t in range(held)
    ]
    for copy in copies + weights:
        copy.start()
    copies[0].wait()
    if first:
        hot = pick[...]
    else:
        copies[1].wait()
        hot = one_hot(scenario_ref, gates_ref.shape[0])
        hot_ref[...] = hot
    hot = jnp.concatenate([hot] * 3, axis=0)
    for i in range(parts):
        part = slice(i * block, (i + 1) * block)
        if not first:
            copies[2 + i].wait()
            for j in range(cols):
                lane = i * block + j * 128
                rows_ref[j] = (
                    pre_ref[:, :, lane : lane + 128].astype(F32).reshape(count * toks, 128)
                )
            for t in range(held, toks):
                rest_ref[t - held, :, part] = take_rows(rows_ref, t, count, toks)
        for t in range(held):
            gate = gates_ref[:, first + t, part]
            high = gate.astype(BF16)
            rest = gate - high.astype(F32)
            mid = rest.astype(BF16)
            low = (rest - mid.astype(F32)).astype(BF16)
            rate = lax.dot_general(
                hot,
                jnp.concatenate([high, mid, low], axis=0),
                (((0,), (0,)), ((), ())),
                preferred_element_type=F32,
            )
            value = source[t, :, part] if first else take_rows(rows_ref, t, count, toks)
            activated, slope = gelu_parts(value)
            h_ref[t, :, part] = (activated * rate).astype(BF16)
            act_ref[t, :, part] = activated
            mul_ref[t, :, part] = rate * slope
    for copy in weights:
        copy.wait()


def activations(first, source, gates, pick, down_weight):
    scen, toks, width = gates.shape
    count = source.shape[1] if first else source.shape[0]
    held = toks // 2
    parts = width // 512
    vmem = pl.BlockSpec(memory_space=pltpu.VMEM)
    hbm = pl.BlockSpec(memory_space=pltpu.HBM)
    shapes = [
        jax.ShapeDtypeStruct((held, count, width), BF16),
        jax.ShapeDtypeStruct((held, count, width), F32),
        jax.ShapeDtypeStruct((held, count, width), F32),
        jax.ShapeDtypeStruct((held,) + down_weight.shape[1:], BF16),
    ]
    scratch = [pltpu.VMEM(gates.shape, F32), pltpu.SemaphoreType.DMA((2 + parts + held,))]
    if not first:
        shapes += [
            jax.ShapeDtypeStruct((scen, count), BF16),
            jax.ShapeDtypeStruct((toks - held, count, width), F32),
        ]
        scratch = [
            pltpu.VMEM((count, toks, width), BF16),
            pltpu.VMEM(pick.shape, jnp.int32),
            pltpu.VMEM((512 // 128, count * toks, 128), F32),
        ] + scratch
        source, pick = pin(source), pin(pick)
    return pl.pallas_call(
        functools.partial(act_kernel, parts, first, toks),
        in_specs=[vmem, hbm, vmem, hbm] if first else [hbm] * 4,
        out_specs=[vmem] * len(shapes),
        out_shape=shapes,
        scratch_shapes=scratch,
        compiler_params=pltpu.CompilerParams(vmem_limit_bytes=14 << 20),
        cost_estimate=pl.CostEstimate(flops=1, bytes_accessed=1, transcendentals=0),
        name="act",
    )(source, pin(gates), pick, pin(down_weight))


def token_kernel(t, at, parts, merge, sources, *refs):
    chunks, refs = refs[:parts], refs[parts:]
    shards = [chunk.at[at] for chunk in chunks]
    all_w, all_act, all_mul, all_h, hot_ref = refs[:5]
    w_ref, act_ref, mul_ref, h_ref = [ref.at[t % 2] for ref in (all_w, all_act, all_mul, all_h)]
    refs = refs[5:]
    if t:
        refs = refs[2:]
    done = ()
    if merge:
        done, refs = refs[:t], refs[t:]
    down_hbm, rows_ref, gate_ref = refs[:3]
    refs = refs[3:]
    if merge:
        pre_ref, refs = refs[0], refs[1:]
    if not t:
        gain_ref, refs = refs[0], refs[1:]
    dz_ref, out_ref, sems = refs[:3]

    me = lax.axis_index("dp")
    size = shards[0].shape[0]
    width = dz_ref.shape[1]
    for k in range(parts):
        place = sum(jnp.where(me == m, sources[m][k], 0) for m in range(parts))
        start = pl.multiple_of(place * size, 16)
        dz_ref[pl.ds(start, size), :] = shards[k][:, :width]
    if not t:
        total = sum(shard[:, width + i : width + i + 128].astype(F32) for shard in shards for i in (0, 128))
        lines_ref = refs[3]
        lines_ref[...] = total
        share = gain_ref.shape[1] // 128
        cols = width // 128
        for i in range(gain_ref.shape[0]):
            for j in range(share):
                gain_ref[i : i + 1, j * 128 : (j + 1) * 128] = lines_ref[
                    pl.ds(i * cols + me * share + j, 1), :
                ]
    dz = dz_ref[...]
    hidden = out_ref.shape[0]
    block = hidden // 3
    hot = hot_ref[...]
    writes = []

    def write(source, target, k):
        writes.append(pltpu.make_async_copy(source, target, sems.at[k]))
        writes[-1].start()

    def down(i):
        rows = pl.ds(i * block, block)
        out_ref[i * block : (i + 1) * block] = lax.dot_general(
            h_ref[:, i * block : (i + 1) * block],
            dz,
            (((0,), (0,)), ((), ())),
            preferred_element_type=F32,
        ).astype(BF16)
        write(out_ref.at[rows], down_hbm.at[t, rows], i)

    def back(i):
        part = slice(i * block, (i + 1) * block)
        d_hidden = lax.dot_general(
            dz, w_ref[part], (((1,), (1,)), ((), ())), preferred_element_type=F32
        )
        product = d_hidden * act_ref[:, part]
        high = product.astype(BF16)
        low = (product - high.astype(F32)).astype(BF16)
        d_gate = jnp.dot(hot, high, preferred_element_type=F32) + jnp.dot(
            hot, low, preferred_element_type=F32
        )
        d_pre = d_hidden * mul_ref[:, part]
        count = d_pre.shape[0]
        toks = rows_ref.shape[1] // count
        cols = block // 128
        put_rows(rows_ref, t, count, toks, d_pre, i * cols)
        if not merge:
            gate_ref[:, part] = d_gate
            return
        spill_ref = refs[3]
        for k in range(t):
            gate_ref[:, k, part] = done[k][:, part]
        gate_ref[:, t, part] = d_gate
        if i > 1:
            writes[2 * i - 3].wait()
        spill(rows_ref.at[i * cols : (i + 1) * cols], spill_ref.at[i % 2])
        write(spill_ref.at[i % 2], pre_ref.at[:, :, pl.ds(i * block, block)], 3 + i)

    for i in range(3):
        down(i)
        back(i)
    for k, copy in enumerate(writes):
        if not merge or k != 1:
            copy.wait()


def token_step(t, at, toks, sources, shards, held, act, mul, h, hot, down, done):
    hidden, width = held.shape[1:]
    scen, count = hot.shape
    parts = len(shards)
    merge = t == toks - 1
    anywhere = pl.BlockSpec(memory_space=pltpu.HBM)
    vmem = pl.BlockSpec(memory_space=pltpu.VMEM)
    operands = list(shards) + [held, act, mul, h, hot]
    specs = [vmem] * (parts + 5)
    aliases = {}
    if t:
        aliases = {len(operands): 0, len(operands) + 1: 1}
        operands += list(down)
        specs += [anywhere, vmem]
    scratch = [
        pltpu.VMEM((count, width), BF16),
        pltpu.VMEM((hidden, width), BF16),
        pltpu.SemaphoreType.DMA((6,)),
    ]
    if merge:
        operands += list(done)
        specs += [vmem] * t
        scratch.append(pltpu.VMEM((2, count, toks, hidden // 3), BF16))
        gate_shape = (scen, toks, hidden)
    else:
        gate_shape = (scen, hidden)
    shapes = [
        jax.ShapeDtypeStruct((toks, hidden, width), BF16),
        jax.ShapeDtypeStruct((hidden // 128, count * toks, 128), F32),
        jax.ShapeDtypeStruct(gate_shape, F32),
    ]
    out_specs = [anywhere, vmem, vmem]
    if merge:
        shapes.append(jax.ShapeDtypeStruct((count, toks, hidden), BF16))
        out_specs.append(anywhere)
    if not t:
        shapes.append(jax.ShapeDtypeStruct((toks, width // parts), F32))
        out_specs.append(vmem)
        scratch.append(pltpu.VMEM((shards[0].shape[1], 128), F32))
    return pl.pallas_call(
        functools.partial(token_kernel, t, at, parts, merge, sources),
        in_specs=specs,
        out_specs=out_specs,
        scratch_shapes=scratch,
        out_shape=shapes,
        input_output_aliases=aliases,
        compiler_params=pltpu.CompilerParams(vmem_limit_bytes=14 << 20),
        cost_estimate=pl.CostEstimate(flops=1, bytes_accessed=1, transcendentals=0),
        name="token",
    )(*operands)


def plain_tokens(dz, pre_act, gates, down_weight, scenario):
    piece = lax.all_gather(dz, "dp", axis=1, tiled=True)
    onehot = (scenario[:, None] == jnp.arange(gates.shape[0], dtype=jnp.int32)[None, :]).astype(F32)
    rate = jnp.einsum("bs,stf->btf", onehot, gates, precision=lax.Precision.HIGHEST)
    activated, slope = gelu_parts(pre_act.astype(F32))
    hidden = (activated * rate).astype(BF16)
    d_hidden = jnp.einsum("tbc,tfc->btf", piece, down_weight, preferred_element_type=F32)
    gate = jnp.einsum("bs,btf->stf", onehot, d_hidden * activated, precision=lax.Precision.HIGHEST)
    pre = (d_hidden * rate * slope).astype(BF16)
    down = jnp.einsum("btf,tbc->tfc", hidden, piece, preferred_element_type=F32).astype(BF16)
    return pre, down, gate


def after(value, *others):
    return lax.optimization_barrier((value, *others))[0]


def swap(send):
    groups = 1 + len(send)
    return [
        lax.ppermute(v, "tok", [(p, p ^ (k + 1)) for p in range(groups)]) for k, v in enumerate(send)
    ]


def ring_tokens(dz, send, pre_act, gates, down_weight, scenario):
    dp = lax.axis_size("dp")
    order = ring_order(dp)
    ring = [(order[k], order[(k + 1) % dp]) for k in range(dp)]
    place = {device: k for k, device in enumerate(order)}
    sources = [[order[(place[m] - s) % dp] for s in range(dp)] for m in range(dp)]
    shards = [[v] for v in dz]

    def hop(i, *others):
        last = shards[i][-1]
        shards[i].append(lax.ppermute(after(last, *others) if others else last, "dp", ring))

    for i in range(4):
        hop(i)
    recv = swap(send)
    h, act, mul, held, hot, rest = [
        [v] for v in activations(0, pre_act, gates, scenario.reshape(1, -1), down_weight)
    ]
    hop(0, h[0])
    hop(1, h[0], shards[2][1])
    hot, rest = hot[0], rest[0]
    more = activations(2, rest, gates, hot, down_weight)
    for have, new in zip((h, act, mul, held), more):
        have.append(new)
    d_input = mix([after(r, h[0]) for r in recv], dz, down_weight.shape[2])
    hop(2)
    hop(3)
    hop(0)
    hop(1, h[1])
    hot = after(hot, d_input)

    down, rows, done = None, None, []
    homes = [(i, k) for i, v in enumerate(dz) for k in range(v.shape[0])]
    for t, (i, at) in enumerate(homes):
        down, rows, gate, *more = token_step(
            t, at, len(homes), sources, shards[i], held[t // 2], act[t // 2], mul[t // 2], h[t // 2], hot, (down, rows), done
        )
        done.append(gate)
        if t == 0:
            gain_gradient = more[0]
            hop(2, gate)
        if t == 1:
            hop(3, gate)
    return d_input, more[0], down, gate, gain_gradient


def per_device(pre_norm, cotangent, gain, pre_act, gates, down_weight, scenario):
    groups = lax.axis_size("tok")
    toks, width = gain.shape
    fits = down_weight.shape[1] == 1536 and toks == 4 and lax.axis_size("dp") == 4
    chunks, spare = ((1, 1, 1, 1), 256) if fits else ((toks,), 0)
    outs = norm(pre_norm, cotangent, gain, groups, chunks, spare)
    dz, send, gain_part = outs[: len(chunks)], outs[len(chunks) : -1], outs[-1]
    if fits:
        return ring_tokens(dz, send, pre_act, gates, down_weight, scenario)
    d_input = mix(swap(send), dz, width)
    pre, down, gate = plain_tokens(dz[0], pre_act, gates, down_weight, scenario)
    gain_gradient = lax.psum_scatter(gain_part, "dp", scatter_dimension=1, tiled=True)
    return d_input, pre, down, gate, gain_gradient


def solution(mesh):
    placed = (
        P(("group", "dp"), "tok", None),
        P(("group", "dp"), "tok", None),
        P("tok", None),
        P("group", "tok", "dp"),
        P(None, "tok", "dp"),
        P("tok", "dp", None),
        P("group"),
    )
    return jax.shard_map(
        per_device,
        mesh=mesh,
        in_specs=placed,
        out_specs=(
            P(("group", "dp"), "tok", None),
            P("group", "tok", "dp"),
            P(("group", "tok"), "dp", None),
            P("group", "tok", "dp"),
            P(("group", "tok"), "dp"),
        ),
        check_vma=False,
    )
```

```python
import functools
import jax
import jax.numpy as jnp
from jax import lax
from jax.experimental import pallas as pl
from jax.experimental.pallas import tpu as pltpu
from jax.sharding import PartitionSpec as P

F32 = jnp.float32
BF16 = jnp.bfloat16
LIMIT = 56 << 20


def gelu_parts(value):
    square = value * value
    tangent = jnp.tanh(value * (0.7978845608 + (0.7978845608 * 0.044715) * square))
    half = 0.5 + 0.5 * tangent
    activated = value * half
    slope = half + activated * (1.0 - tangent) * (
        0.7978845608 + (0.7978845608 * 3.0 * 0.044715) * square
    )
    return activated, slope


def pin(value):
    return pltpu.with_memory_space_constraint(value, pltpu.HBM)


def ring_order(count):
    return [0] + list(range(1, count, 2)) + list(range(2, count, 2))[::-1]


def take_rows(rows_ref, t, count, toks):
    return jnp.concatenate(
        [rows_ref[j, pl.ds(t, count, stride=toks), :] for j in range(rows_ref.shape[0])], axis=1
    )


def put_rows(rows_ref, t, count, toks, value, first=0):
    for j in range(value.shape[1] // 128):
        rows_ref[first + j, pl.ds(t, count, stride=toks), :] = value[:, j * 128 : (j + 1) * 128]


def spill(rows_ref, out_ref):
    count, toks, width = out_ref.shape
    for j in range(width // 128):
        out_ref[:, :, j * 128 : (j + 1) * 128] = (
            rows_ref[j].reshape(count, toks, 128).astype(out_ref.dtype)
        )


def norm_kernel(pieces, chunks, x_hbm, g_hbm, gain_hbm, *refs):
    dz_refs, refs = refs[:chunks], refs[chunks:]
    send_refs, (gg_ref, x_ref, g_ref, gain_ref, rows_ref, sems) = refs[:-6], refs[-6:]
    count, toks, width = x_ref.shape
    gain_copy = pltpu.make_async_copy(gain_hbm, gain_ref, sems.at[2 * pieces])
    gain_copy.start()
    size = count // pieces
    copies = []
    for k in range(pieces):
        part = pl.ds(k * size, size)
        pair = (
            pltpu.make_async_copy(x_hbm.at[part], x_ref.at[part], sems.at[2 * k]),
            pltpu.make_async_copy(g_hbm.at[part], g_ref.at[part], sems.at[2 * k + 1]),
        )
        for copy in pair:
            copy.start()
        copies.append(pair)
    gain_copy.wait()
    step = 8 // toks
    gain = jnp.concatenate([gain_ref[...]] * step, axis=0)
    scale = 1.0 / width
    total = jnp.zeros((8, width), F32)
    for i in range(count // step):
        if i * step % size == 0:
            for copy in copies[i * step // size]:
                copy.wait()
        x = x_ref[i * step : (i + 1) * step].astype(F32).reshape(8, width)
        ct = g_ref[i * step : (i + 1) * step].astype(F32).reshape(8, width)
        g = ct * gain
        c = x - jnp.sum(x, axis=-1, keepdims=True) * scale
        mean_g = jnp.sum(g, axis=-1, keepdims=True) * scale
        rstd = lax.rsqrt(jnp.sum(c * c, axis=-1, keepdims=True) * scale + 1e-05)
        mean_gc = jnp.sum(g * c, axis=-1, keepdims=True) * scale
        xhat = c * rstd
        total = total + ct * xhat
        dz = rstd * (g - mean_g - xhat * (mean_gc * rstd))
        for j in range(width // 128):
            rows_ref[j, i * 8 : (i + 1) * 8, :] = dz[:, j * 128 : (j + 1) * 128]
    part = sum(total[k * toks : (k + 1) * toks] for k in range(step))
    gg_ref[...] = part
    dz = [ref.at[i] for ref in dz_refs for i in range(ref.shape[0])]
    for t in range(toks):
        dz[t][:, :width] = take_rows(rows_ref, t, count, toks).astype(BF16)
    if dz[0].shape[1] > width:
        high = part.astype(BF16).astype(F32)
        for k, value in enumerate((high, part - high)):
            lines = [
                value[i : i + 1, j : j + 128] for i in range(toks) for j in range(0, width, 128)
            ]
            dz[0][:, width + 128 * k : width + 128 * (k + 1)] = jnp.concatenate(
                lines, axis=0
            ).astype(BF16)
    me = lax.axis_index("tok")
    block = width // (1 + len(send_refs))
    for k, send_ref in enumerate(send_refs):
        start = pl.multiple_of((me ^ (k + 1)) * block, 128)
        for t in range(toks):
            send_ref[t] = dz[t][:, pl.ds(start, block)]


def norm(pre_norm, cotangent, gain, groups, chunks, spare):
    count, toks, width = pre_norm.shape
    pieces = 4
    return pl.pallas_call(
        functools.partial(norm_kernel, pieces, len(chunks)),
        out_shape=[
            jax.ShapeDtypeStruct((size, count, width + (0 if i else spare)), BF16)
            for i, size in enumerate(chunks)
        ]
        + [jax.ShapeDtypeStruct((toks, count, width // groups), BF16)] * (groups - 1)
        + [jax.ShapeDtypeStruct((toks, width), F32)],
        in_specs=[pl.BlockSpec(memory_space=pltpu.HBM)] * 3,
        out_specs=[pl.BlockSpec(memory_space=pltpu.VMEM)] * (len(chunks) + groups),
        scratch_shapes=[
            pltpu.VMEM((count, toks, width), BF16),
            pltpu.VMEM((count, toks, width), BF16),
            pltpu.VMEM((toks, width), F32),
            pltpu.VMEM((width // 128, count * toks, 128), F32),
            pltpu.SemaphoreType.DMA((2 * pieces + 1,)),
        ],
        compiler_params=pltpu.CompilerParams(vmem_limit_bytes=12 << 20),
        name="norm",
    )(pin(pre_norm), pin(cotangent), pin(gain))


def mix_kernel(groups, *refs):
    recv_refs, dz_refs, (out_ref, rows_ref) = refs[: groups - 1], refs[groups - 1 : -2], refs[-2:]
    dz_refs = [ref.at[i] for ref in dz_refs for i in range(ref.shape[0])]
    count, toks, width = out_ref.shape
    block = width // (1 + len(recv_refs))
    piece = block // toks
    me = lax.axis_index("tok")
    for k in range(1 + len(recv_refs)):
        start = pl.multiple_of((me ^ k) * block, 128)
        if k:
            got = [recv_refs[k - 1][i].astype(F32) for i in range(toks)]
        else:
            got = [dz_refs[i][:, pl.ds(start, block)].astype(F32) for i in range(toks)]
        for j in range(toks):
            mixed = jnp.concatenate(
                [got[i][:, j * piece : (j + 1) * piece] for i in range(toks)], axis=1
            )
            mixed = mixed + dz_refs[j][:, pl.ds(start, block)].astype(F32)
            put_rows(rows_ref, j, count, toks, mixed, (me ^ k) * (block // 128))
    spill(rows_ref, out_ref)


def mix(recv, dz, width):
    toks = sum(v.shape[0] for v in dz)
    count = dz[0].shape[1]
    return pl.pallas_call(
        functools.partial(mix_kernel, 1 + len(recv)),
        out_shape=jax.ShapeDtypeStruct((count, toks, width), BF16),
        in_specs=[pl.BlockSpec(memory_space=pltpu.VMEM)] * (len(recv) + len(dz)),
        out_specs=pl.BlockSpec(memory_space=pltpu.VMEM),
        scratch_shapes=[pltpu.VMEM((width // 128, count * toks, 128), F32)],
        compiler_params=pltpu.CompilerParams(vmem_limit_bytes=8 << 20),
        cost_estimate=pl.CostEstimate(flops=1, bytes_accessed=1, transcendentals=0),
        name="mix",
    )(*recv, *dz)


def one_hot(scenario_ref, count):
    return (
        lax.broadcasted_iota(jnp.int32, (count, scenario_ref.shape[1]), 0) == scenario_ref[...]
    ).astype(BF16)


def act_kernel(parts, first, toks, source, gates_hbm, pick, w_hbm, *refs):
    h_ref, act_ref, mul_ref, w_ref, refs = *refs[:4], refs[4:]
    count, width = act_ref.shape[1:]
    held = act_ref.shape[0]
    block = width // parts
    cols = block // 128
    if not first:
        hot_ref, rest_ref, pre_ref, scenario_ref, rows_ref, *refs = refs
    gates_ref, sems = refs
    copies = [pltpu.make_async_copy(gates_hbm, gates_ref, sems.at[0])]
    if not first:
        copies.append(pltpu.make_async_copy(pick, scenario_ref, sems.at[1]))
        for i in range(parts):
            part = pl.ds(i * block, block)
            copies.append(
                pltpu.make_async_copy(source.at[:, :, part], pre_ref.at[:, :, part], sems.at[2 + i])
            )
    weights = [
        pltpu.make_async_copy(w_hbm.at[first + t], w_ref.at[t], sems.at[2 + parts + t])
        for t in range(held)
    ]
    for copy in copies + weights:
        copy.start()
    copies[0].wait()
    if first:
        hot = pick[...]
    else:
        copies[1].wait()
        hot = one_hot(scenario_ref, gates_ref.shape[0])
        hot_ref[...] = hot
    hot = jnp.concatenate([hot] * 3, axis=0)
    for i in range(parts):
        part = slice(i * block, (i + 1) * block)
        if not first:
            copies[2 + i].wait()
            for j in range(cols):
                lane = i * block + j * 128
                rows_ref[j] = (
                    pre_ref[:, :, lane : lane + 128].astype(F32).reshape(count * toks, 128)
                )
            for t in range(held, toks):
                rest_ref[t - held, :, part] = take_rows(rows_ref, t, count, toks)
        for t in range(held):
            gate = gates_ref[:, first + t, part]
            high = gate.astype(BF16)
            rest = gate - high.astype(F32)
            mid = rest.astype(BF16)
            low = (rest - mid.astype(F32)).astype(BF16)
            rate = lax.dot_general(
                hot,
                jnp.concatenate([high, mid, low], axis=0),
                (((0,), (0,)), ((), ())),
                preferred_element_type=F32,
            )
            value = source[t, :, part] if first else take_rows(rows_ref, t, count, toks)
            activated, slope = gelu_parts(value)
            h_ref[t, :, part] = (activated * rate).astype(BF16)
            act_ref[t, :, part] = activated
            mul_ref[t, :, part] = rate * slope
    for copy in weights:
        copy.wait()


def activations(first, source, gates, pick, down_weight):
    scen, toks, width = gates.shape
    count = source.shape[1] if first else source.shape[0]
    held = toks // 2
    parts = width // 512
    vmem = pl.BlockSpec(memory_space=pltpu.VMEM)
    hbm = pl.BlockSpec(memory_space=pltpu.HBM)
    shapes = [
        jax.ShapeDtypeStruct((held, count, width), BF16),
        jax.ShapeDtypeStruct((held, count, width), F32),
        jax.ShapeDtypeStruct((held, count, width), F32),
        jax.ShapeDtypeStruct((held,) + down_weight.shape[1:], BF16),
    ]
    scratch = [pltpu.VMEM(gates.shape, F32), pltpu.SemaphoreType.DMA((2 + parts + held,))]
    if not first:
        shapes += [
            jax.ShapeDtypeStruct((scen, count), BF16),
            jax.ShapeDtypeStruct((toks - held, count, width), F32),
        ]
        scratch = [
            pltpu.VMEM((count, toks, width), BF16),
            pltpu.VMEM(pick.shape, jnp.int32),
            pltpu.VMEM((512 // 128, count * toks, 128), F32),
        ] + scratch
        source, pick = pin(source), pin(pick)
    return pl.pallas_call(
        functools.partial(act_kernel, parts, first, toks),
        in_specs=[vmem, hbm, vmem, hbm] if first else [hbm] * 4,
        out_specs=[vmem] * len(shapes),
        out_shape=shapes,
        scratch_shapes=scratch,
        compiler_params=pltpu.CompilerParams(vmem_limit_bytes=14 << 20),
        cost_estimate=pl.CostEstimate(flops=1, bytes_accessed=1, transcendentals=0),
        name="act",
    )(source, pin(gates), pick, pin(down_weight))


def token_kernel(t, at, parts, merge, sources, *refs):
    chunks, refs = refs[:parts], refs[parts:]
    shards = [chunk.at[at] for chunk in chunks]
    all_w, all_act, all_mul, all_h, hot_ref = refs[:5]
    w_ref, act_ref, mul_ref, h_ref = [ref.at[t % 2] for ref in (all_w, all_act, all_mul, all_h)]
    refs = refs[5:]
    if t:
        refs = refs[2:]
    done = ()
    if merge:
        done, refs = refs[:t], refs[t:]
    down_hbm, rows_ref, gate_ref = refs[:3]
    refs = refs[3:]
    if merge:
        pre_ref, refs = refs[0], refs[1:]
    if not t:
        gain_ref, refs = refs[0], refs[1:]
    dz_ref, out_ref, sems = refs[:3]

    me = lax.axis_index("dp")
    size = shards[0].shape[0]
    width = dz_ref.shape[1]
    for k in range(parts):
        place = sum(jnp.where(me == m, sources[m][k], 0) for m in range(parts))
        start = pl.multiple_of(place * size, 16)
        dz_ref[pl.ds(start, size), :] = shards[k][:, :width]
    if not t:
        total = sum(shard[:, width + i : width + i + 128].astype(F32) for shard in shards for i in (0, 128))
        lines_ref = refs[3]
        lines_ref[...] = total
        share = gain_ref.shape[1] // 128
        cols = width // 128
        for i in range(gain_ref.shape[0]):
            for j in range(share):
                gain_ref[i : i + 1, j * 128 : (j + 1) * 128] = lines_ref[
                    pl.ds(i * cols + me * share + j, 1), :
                ]
    dz = dz_ref[...]
    hidden = out_ref.shape[0]
    block = hidden // 3
    hot = hot_ref[...]
    writes = []

    def write(source, target, k):
        writes.append(pltpu.make_async_copy(source, target, sems.at[k]))
        writes[-1].start()

    def down(i):
        rows = pl.ds(i * block, block)
        out_ref[i * block : (i + 1) * block] = lax.dot_general(
            h_ref[:, i * block : (i + 1) * block],
            dz,
            (((0,), (0,)), ((), ())),
            preferred_element_type=F32,
        ).astype(BF16)
        write(out_ref.at[rows], down_hbm.at[t, rows], i)

    def back(i):
        part = slice(i * block, (i + 1) * block)
        d_hidden = lax.dot_general(
            dz, w_ref[part], (((1,), (1,)), ((), ())), preferred_element_type=F32
        )
        product = d_hidden * act_ref[:, part]
        high = product.astype(BF16)
        low = (product - high.astype(F32)).astype(BF16)
        d_gate = jnp.dot(hot, high, preferred_element_type=F32) + jnp.dot(
            hot, low, preferred_element_type=F32
        )
        d_pre = d_hidden * mul_ref[:, part]
        count = d_pre.shape[0]
        toks = rows_ref.shape[1] // count
        cols = block // 128
        put_rows(rows_ref, t, count, toks, d_pre, i * cols)
        if not merge:
            gate_ref[:, part] = d_gate
            return
        spill_ref = refs[3]
        for k in range(t):
            gate_ref[:, k, part] = done[k][:, part]
        gate_ref[:, t, part] = d_gate
        if i > 1:
            writes[2 * i - 3].wait()
        spill(rows_ref.at[i * cols : (i + 1) * cols], spill_ref.at[i % 2])
        write(spill_ref.at[i % 2], pre_ref.at[:, :, pl.ds(i * block, block)], 3 + i)

    for i in range(3):
        down(i)
        back(i)
    for k, copy in enumerate(writes):
        if not merge or k != 1:
            copy.wait()


def token_step(t, at, toks, sources, shards, held, act, mul, h, hot, down, done):
    hidden, width = held.shape[1:]
    scen, count = hot.shape
    parts = len(shards)
    merge = t == toks - 1
    anywhere = pl.BlockSpec(memory_space=pltpu.HBM)
    vmem = pl.BlockSpec(memory_space=pltpu.VMEM)
    operands = list(shards) + [held, act, mul, h, hot]
    specs = [vmem] * (parts + 5)
    aliases = {}
    if t:
        aliases = {len(operands): 0, len(operands) + 1: 1}
        operands += list(down)
        specs += [anywhere, vmem]
    scratch = [
        pltpu.VMEM((count, width), BF16),
        pltpu.VMEM((hidden, width), BF16),
        pltpu.SemaphoreType.DMA((6,)),
    ]
    if merge:
        operands += list(done)
        specs += [vmem] * t
        scratch.append(pltpu.VMEM((2, count, toks, hidden // 3), BF16))
        gate_shape = (scen, toks, hidden)
    else:
        gate_shape = (scen, hidden)
    shapes = [
        jax.ShapeDtypeStruct((toks, hidden, width), BF16),
        jax.ShapeDtypeStruct((hidden // 128, count * toks, 128), F32),
        jax.ShapeDtypeStruct(gate_shape, F32),
    ]
    out_specs = [anywhere, vmem, vmem]
    if merge:
        shapes.append(jax.ShapeDtypeStruct((count, toks, hidden), BF16))
        out_specs.append(anywhere)
    if not t:
        shapes.append(jax.ShapeDtypeStruct((toks, width // parts), F32))
        out_specs.append(vmem)
        scratch.append(pltpu.VMEM((shards[0].shape[1], 128), F32))
    return pl.pallas_call(
        functools.partial(token_kernel, t, at, parts, merge, sources),
        in_specs=specs,
        out_specs=out_specs,
        scratch_shapes=scratch,
        out_shape=shapes,
        input_output_aliases=aliases,
        compiler_params=pltpu.CompilerParams(vmem_limit_bytes=14 << 20),
        cost_estimate=pl.CostEstimate(flops=1, bytes_accessed=1, transcendentals=0),
        name="token",
    )(*operands)


def plain_tokens(dz, pre_act, gates, down_weight, scenario):
    piece = lax.all_gather(dz, "dp", axis=1, tiled=True)
    onehot = (scenario[:, None] == jnp.arange(gates.shape[0], dtype=jnp.int32)[None, :]).astype(F32)
    rate = jnp.einsum("bs,stf->btf", onehot, gates, precision=lax.Precision.HIGHEST)
    activated, slope = gelu_parts(pre_act.astype(F32))
    hidden = (activated * rate).astype(BF16)
    d_hidden = jnp.einsum("tbc,tfc->btf", piece, down_weight, preferred_element_type=F32)
    gate = jnp.einsum("bs,btf->stf", onehot, d_hidden * activated, precision=lax.Precision.HIGHEST)
    pre = (d_hidden * rate * slope).astype(BF16)
    down = jnp.einsum("btf,tbc->tfc", hidden, piece, preferred_element_type=F32).astype(BF16)
    return pre, down, gate


def after(value, *others):
    return lax.optimization_barrier((value, *others))[0]


def swap(send):
    groups = 1 + len(send)
    return [
        lax.ppermute(v, "tok", [(p, p ^ (k + 1)) for p in range(groups)]) for k, v in enumerate(send)
    ]


def ring_tokens(dz, send, pre_act, gates, down_weight, scenario):
    dp = lax.axis_size("dp")
    order = ring_order(dp)
    ring = [(order[k], order[(k + 1) % dp]) for k in range(dp)]
    place = {device: k for k, device in enumerate(order)}
    sources = [[order[(place[m] - s) % dp] for s in range(dp)] for m in range(dp)]
    shards = [[v] for v in dz]

    def hop(i, *others):
        last = shards[i][-1]
        shards[i].append(lax.ppermute(after(last, *others) if others else last, "dp", ring))

    for i in range(4):
        hop(i)
    recv = swap(send)
    h, act, mul, held, hot, rest = [
        [v] for v in activations(0, pre_act, gates, scenario.reshape(1, -1), down_weight)
    ]
    hop(0, h[0])
    hop(1, h[0], shards[2][1])
    hot, rest = hot[0], rest[0]
    more = activations(2, rest, gates, hot, down_weight)
    for have, new in zip((h, act, mul, held), more):
        have.append(new)
    d_input = mix([after(r, h[0]) for r in recv], dz, down_weight.shape[2])
    hop(2, h[1])
    hop(3)
    hop(0)
    hop(1)
    hot = after(hot, d_input)

    down, rows, done = None, None, []
    homes = [(i, k) for i, v in enumerate(dz) for k in range(v.shape[0])]
    for t, (i, at) in enumerate(homes):
        down, rows, gate, *more = token_step(
            t, at, len(homes), sources, shards[i], held[t // 2], act[t // 2], mul[t // 2], h[t // 2], hot, (down, rows), done
        )
        done.append(gate)
        if t == 0:
            gain_gradient = more[0]
            hop(2, gate)
        if t == 1:
            hop(3, gate)
    return d_input, more[0], down, gate, gain_gradient


def per_device(pre_norm, cotangent, gain, pre_act, gates, down_weight, scenario):
    groups = lax.axis_size("tok")
    toks, width = gain.shape
    fits = down_weight.shape[1] == 1536 and toks == 4 and lax.axis_size("dp") == 4
    chunks, spare = ((1, 1, 1, 1), 256) if fits else ((toks,), 0)
    outs = norm(pre_norm, cotangent, gain, groups, chunks, spare)
    dz, send, gain_part = outs[: len(chunks)], outs[len(chunks) : -1], outs[-1]
    if fits:
        return ring_tokens(dz, send, pre_act, gates, down_weight, scenario)
    d_input = mix(swap(send), dz, width)
    pre, down, gate = plain_tokens(dz[0], pre_act, gates, down_weight, scenario)
    gain_gradient = lax.psum_scatter(gain_part, "dp", scatter_dimension=1, tiled=True)
    return d_input, pre, down, gate, gain_gradient


def solution(mesh):
    placed = (
        P(("group", "dp"), "tok", None),
        P(("group", "dp"), "tok", None),
        P("tok", None),
        P("group", "tok", "dp"),
        P(None, "tok", "dp"),
        P("tok", "dp", None),
        P("group"),
    )
    return jax.shard_map(
        per_device,
        mesh=mesh,
        in_specs=placed,
        out_specs=(
            P(("group", "dp"), "tok", None),
            P("group", "tok", "dp"),
            P(("group", "tok"), "dp", None),
            P("group", "tok", "dp"),
            P(("group", "tok"), "dp"),
        ),
        check_vma=False,
    )
```

```python
import functools
import jax
import jax.numpy as jnp
from jax import lax
from jax.experimental import pallas as pl
from jax.experimental.pallas import tpu as pltpu
from jax.sharding import PartitionSpec as P

F32 = jnp.float32
BF16 = jnp.bfloat16
LIMIT = 56 << 20


def gelu_parts(value):
    square = value * value
    tangent = jnp.tanh(value * (0.7978845608 + (0.7978845608 * 0.044715) * square))
    half = 0.5 + 0.5 * tangent
    activated = value * half
    slope = half + activated * (1.0 - tangent) * (
        0.7978845608 + (0.7978845608 * 3.0 * 0.044715) * square
    )
    return activated, slope


def pin(value):
    return pltpu.with_memory_space_constraint(value, pltpu.HBM)


def ring_order(count):
    return [0] + list(range(1, count, 2)) + list(range(2, count, 2))[::-1]


def take_rows(rows_ref, t, count, toks):
    return jnp.concatenate(
        [rows_ref[j, pl.ds(t, count, stride=toks), :] for j in range(rows_ref.shape[0])], axis=1
    )


def put_rows(rows_ref, t, count, toks, value, first=0):
    for j in range(value.shape[1] // 128):
        rows_ref[first + j, pl.ds(t, count, stride=toks), :] = value[:, j * 128 : (j + 1) * 128]


def spill(rows_ref, out_ref):
    count, toks, width = out_ref.shape
    for j in range(width // 128):
        out_ref[:, :, j * 128 : (j + 1) * 128] = (
            rows_ref[j].reshape(count, toks, 128).astype(out_ref.dtype)
        )


def norm_kernel(pieces, chunks, x_hbm, g_hbm, gain_hbm, *refs):
    dz_refs, refs = refs[:chunks], refs[chunks:]
    send_refs, (gg_ref, x_ref, g_ref, gain_ref, rows_ref, sems) = refs[:-6], refs[-6:]
    count, toks, width = x_ref.shape
    gain_copy = pltpu.make_async_copy(gain_hbm, gain_ref, sems.at[2 * pieces])
    gain_copy.start()
    size = count // pieces
    copies = []
    for k in range(pieces):
        part = pl.ds(k * size, size)
        pair = (
            pltpu.make_async_copy(x_hbm.at[part], x_ref.at[part], sems.at[2 * k]),
            pltpu.make_async_copy(g_hbm.at[part], g_ref.at[part], sems.at[2 * k + 1]),
        )
        for copy in pair:
            copy.start()
        copies.append(pair)
    gain_copy.wait()
    step = 8 // toks
    gain = jnp.concatenate([gain_ref[...]] * step, axis=0)
    scale = 1.0 / width
    total = jnp.zeros((8, width), F32)
    for i in range(count // step):
        if i * step % size == 0:
            for copy in copies[i * step // size]:
                copy.wait()
        x = x_ref[i * step : (i + 1) * step].astype(F32).reshape(8, width)
        ct = g_ref[i * step : (i + 1) * step].astype(F32).reshape(8, width)
        g = ct * gain
        c = x - jnp.sum(x, axis=-1, keepdims=True) * scale
        mean_g = jnp.sum(g, axis=-1, keepdims=True) * scale
        rstd = lax.rsqrt(jnp.sum(c * c, axis=-1, keepdims=True) * scale + 1e-05)
        mean_gc = jnp.sum(g * c, axis=-1, keepdims=True) * scale
        xhat = c * rstd
        total = total + ct * xhat
        dz = rstd * (g - mean_g - xhat * (mean_gc * rstd))
        for j in range(width // 128):
            rows_ref[j, i * 8 : (i + 1) * 8, :] = dz[:, j * 128 : (j + 1) * 128]
    part = sum(total[k * toks : (k + 1) * toks] for k in range(step))
    gg_ref[...] = part
    dz = [ref.at[i] for ref in dz_refs for i in range(ref.shape[0])]
    for t in range(toks):
        dz[t][:, :width] = take_rows(rows_ref, t, count, toks).astype(BF16)
    if dz[0].shape[1] > width:
        high = part.astype(BF16).astype(F32)
        for k, value in enumerate((high, part - high)):
            lines = [
                value[i : i + 1, j : j + 128] for i in range(toks) for j in range(0, width, 128)
            ]
            dz[0][:, width + 128 * k : width + 128 * (k + 1)] = jnp.concatenate(
                lines, axis=0
            ).astype(BF16)
    me = lax.axis_index("tok")
    block = width // (1 + len(send_refs))
    for k, send_ref in enumerate(send_refs):
        start = pl.multiple_of((me ^ (k + 1)) * block, 128)
        for t in range(toks):
            send_ref[t] = dz[t][:, pl.ds(start, block)]


def norm(pre_norm, cotangent, gain, groups, chunks, spare):
    count, toks, width = pre_norm.shape
    pieces = 4
    return pl.pallas_call(
        functools.partial(norm_kernel, pieces, len(chunks)),
        out_shape=[
            jax.ShapeDtypeStruct((size, count, width + (0 if i else spare)), BF16)
            for i, size in enumerate(chunks)
        ]
        + [jax.ShapeDtypeStruct((toks, count, width // groups), BF16)] * (groups - 1)
        + [jax.ShapeDtypeStruct((toks, width), F32)],
        in_specs=[pl.BlockSpec(memory_space=pltpu.HBM)] * 3,
        out_specs=[pl.BlockSpec(memory_space=pltpu.VMEM)] * (len(chunks) + groups),
        scratch_shapes=[
            pltpu.VMEM((count, toks, width), BF16),
            pltpu.VMEM((count, toks, width), BF16),
            pltpu.VMEM((toks, width), F32),
            pltpu.VMEM((width // 128, count * toks, 128), F32),
            pltpu.SemaphoreType.DMA((2 * pieces + 1,)),
        ],
        compiler_params=pltpu.CompilerParams(vmem_limit_bytes=12 << 20),
        name="norm",
    )(pin(pre_norm), pin(cotangent), pin(gain))


def mix_kernel(groups, *refs):
    recv_refs, dz_refs, (out_ref, rows_ref) = refs[: groups - 1], refs[groups - 1 : -2], refs[-2:]
    dz_refs = [ref.at[i] for ref in dz_refs for i in range(ref.shape[0])]
    count, toks, width = out_ref.shape
    block = width // (1 + len(recv_refs))
    piece = block // toks
    me = lax.axis_index("tok")
    for k in range(1 + len(recv_refs)):
        start = pl.multiple_of((me ^ k) * block, 128)
        if k:
            got = [recv_refs[k - 1][i].astype(F32) for i in range(toks)]
        else:
            got = [dz_refs[i][:, pl.ds(start, block)].astype(F32) for i in range(toks)]
        for j in range(toks):
            mixed = jnp.concatenate(
                [got[i][:, j * piece : (j + 1) * piece] for i in range(toks)], axis=1
            )
            mixed = mixed + dz_refs[j][:, pl.ds(start, block)].astype(F32)
            put_rows(rows_ref, j, count, toks, mixed, (me ^ k) * (block // 128))
    spill(rows_ref, out_ref)


def mix(recv, dz, width):
    toks = sum(v.shape[0] for v in dz)
    count = dz[0].shape[1]
    return pl.pallas_call(
        functools.partial(mix_kernel, 1 + len(recv)),
        out_shape=jax.ShapeDtypeStruct((count, toks, width), BF16),
        in_specs=[pl.BlockSpec(memory_space=pltpu.VMEM)] * (len(recv) + len(dz)),
        out_specs=pl.BlockSpec(memory_space=pltpu.VMEM),
        scratch_shapes=[pltpu.VMEM((width // 128, count * toks, 128), F32)],
        compiler_params=pltpu.CompilerParams(vmem_limit_bytes=8 << 20),
        cost_estimate=pl.CostEstimate(flops=1, bytes_accessed=1, transcendentals=0),
        name="mix",
    )(*recv, *dz)


def one_hot(scenario_ref, count):
    return (
        lax.broadcasted_iota(jnp.int32, (count, scenario_ref.shape[1]), 0) == scenario_ref[...]
    ).astype(BF16)


def act_kernel(parts, first, toks, source, gates_hbm, pick, w_hbm, *refs):
    h_ref, act_ref, mul_ref, w_ref, refs = *refs[:4], refs[4:]
    count, width = act_ref.shape[1:]
    held = act_ref.shape[0]
    block = width // parts
    cols = block // 128
    if not first:
        hot_ref, rest_ref, pre_ref, scenario_ref, rows_ref, *refs = refs
    gates_ref, sems = refs
    copies = [pltpu.make_async_copy(gates_hbm, gates_ref, sems.at[0])]
    if not first:
        copies.append(pltpu.make_async_copy(pick, scenario_ref, sems.at[1]))
        for i in range(parts):
            part = pl.ds(i * block, block)
            copies.append(
                pltpu.make_async_copy(source.at[:, :, part], pre_ref.at[:, :, part], sems.at[2 + i])
            )
    weights = [
        pltpu.make_async_copy(w_hbm.at[first + t], w_ref.at[t], sems.at[2 + parts + t])
        for t in range(held)
    ]
    for copy in copies + weights:
        copy.start()
    copies[0].wait()
    if first:
        hot = pick[...]
    else:
        copies[1].wait()
        hot = one_hot(scenario_ref, gates_ref.shape[0])
        hot_ref[...] = hot
    hot = jnp.concatenate([hot] * 3, axis=0)
    for i in range(parts):
        part = slice(i * block, (i + 1) * block)
        if not first:
            copies[2 + i].wait()
            for j in range(cols):
                lane = i * block + j * 128
                rows_ref[j] = (
                    pre_ref[:, :, lane : lane + 128].astype(F32).reshape(count * toks, 128)
                )
            for t in range(held, toks):
                rest_ref[t - held, :, part] = take_rows(rows_ref, t, count, toks)
        for t in range(held):
            gate = gates_ref[:, first + t, part]
            high = gate.astype(BF16)
            rest = gate - high.astype(F32)
            mid = rest.astype(BF16)
            low = (rest - mid.astype(F32)).astype(BF16)
            rate = lax.dot_general(
                hot,
                jnp.concatenate([high, mid, low], axis=0),
                (((0,), (0,)), ((), ())),
                preferred_element_type=F32,
            )
            value = source[t, :, part] if first else take_rows(rows_ref, t, count, toks)
            activated, slope = gelu_parts(value)
            h_ref[t, :, part] = (activated * rate).astype(BF16)
            act_ref[t, :, part] = activated
            mul_ref[t, :, part] = rate * slope
    for copy in weights:
        copy.wait()


def activations(first, source, gates, pick, down_weight):
    scen, toks, width = gates.shape
    count = source.shape[1] if first else source.shape[0]
    held = toks // 2
    parts = width // 512
    vmem = pl.BlockSpec(memory_space=pltpu.VMEM)
    hbm = pl.BlockSpec(memory_space=pltpu.HBM)
    shapes = [
        jax.ShapeDtypeStruct((held, count, width), BF16),
        jax.ShapeDtypeStruct((held, count, width), F32),
        jax.ShapeDtypeStruct((held, count, width), F32),
        jax.ShapeDtypeStruct((held,) + down_weight.shape[1:], BF16),
    ]
    scratch = [pltpu.VMEM(gates.shape, F32), pltpu.SemaphoreType.DMA((2 + parts + held,))]
    if not first:
        shapes += [
            jax.ShapeDtypeStruct((scen, count), BF16),
            jax.ShapeDtypeStruct((toks - held, count, width), F32),
        ]
        scratch = [
            pltpu.VMEM((count, toks, width), BF16),
            pltpu.VMEM(pick.shape, jnp.int32),
            pltpu.VMEM((512 // 128, count * toks, 128), F32),
        ] + scratch
        source, pick = pin(source), pin(pick)
    return pl.pallas_call(
        functools.partial(act_kernel, parts, first, toks),
        in_specs=[vmem, hbm, vmem, hbm] if first else [hbm] * 4,
        out_specs=[vmem] * len(shapes),
        out_shape=shapes,
        scratch_shapes=scratch,
        compiler_params=pltpu.CompilerParams(vmem_limit_bytes=14 << 20),
        cost_estimate=pl.CostEstimate(flops=1, bytes_accessed=1, transcendentals=0),
        name="act",
    )(source, pin(gates), pick, pin(down_weight))


def token_kernel(t, at, parts, merge, sources, *refs):
    chunks, refs = refs[:parts], refs[parts:]
    shards = [chunk.at[at] for chunk in chunks]
    all_w, all_act, all_mul, all_h, hot_ref = refs[:5]
    w_ref, act_ref, mul_ref, h_ref = [ref.at[t % 2] for ref in (all_w, all_act, all_mul, all_h)]
    refs = refs[5:]
    if t:
        refs = refs[2:]
    done = ()
    if merge:
        done, refs = refs[:t], refs[t:]
    down_hbm, rows_ref, gate_ref = refs[:3]
    refs = refs[3:]
    if merge:
        pre_ref, refs = refs[0], refs[1:]
    if not t:
        gain_ref, refs = refs[0], refs[1:]
    dz_ref, out_ref, sems = refs[:3]

    me = lax.axis_index("dp")
    size = shards[0].shape[0]
    width = dz_ref.shape[1]
    for k in range(parts):
        place = sum(jnp.where(me == m, sources[m][k], 0) for m in range(parts))
        start = pl.multiple_of(place * size, 16)
        dz_ref[pl.ds(start, size), :] = shards[k][:, :width]
    dz = dz_ref[...]
    hidden = out_ref.shape[0]
    block = hidden // 3
    hot = hot_ref[...]
    writes = []

    def write(source, target, k):
        writes.append(pltpu.make_async_copy(source, target, sems.at[k]))
        writes[-1].start()

    def down(i):
        rows = pl.ds(i * block, block)
        out_ref[i * block : (i + 1) * block] = lax.dot_general(
            h_ref[:, i * block : (i + 1) * block],
            dz,
            (((0,), (0,)), ((), ())),
            preferred_element_type=F32,
        ).astype(BF16)
        write(out_ref.at[rows], down_hbm.at[t, rows], i)

    def back(i):
        part = slice(i * block, (i + 1) * block)
        d_hidden = lax.dot_general(
            dz, w_ref[part], (((1,), (1,)), ((), ())), preferred_element_type=F32
        )
        product = d_hidden * act_ref[:, part]
        high = product.astype(BF16)
        low = (product - high.astype(F32)).astype(BF16)
        d_gate = jnp.dot(hot, high, preferred_element_type=F32) + jnp.dot(
            hot, low, preferred_element_type=F32
        )
        d_pre = d_hidden * mul_ref[:, part]
        count = d_pre.shape[0]
        toks = rows_ref.shape[1] // count
        cols = block // 128
        put_rows(rows_ref, t, count, toks, d_pre, i * cols)
        if not merge:
            gate_ref[:, part] = d_gate
            return
        spill_ref = refs[3]
        for k in range(t):
            gate_ref[:, k, part] = done[k][:, part]
        gate_ref[:, t, part] = d_gate
        if i > 1:
            writes[2 * i - 3].wait()
        spill(rows_ref.at[i * cols : (i + 1) * cols], spill_ref.at[i % 2])
        write(spill_ref.at[i % 2], pre_ref.at[:, :, pl.ds(i * block, block)], 3 + i)

    def gain():
        total = sum(shard[:, width + i : width + i + 128].astype(F32) for shard in shards for i in (0, 128))
        lines_ref = refs[3]
        lines_ref[...] = total
        share = gain_ref.shape[1] // 128
        cols = width // 128
        for i in range(gain_ref.shape[0]):
            for j in range(share):
                gain_ref[i : i + 1, j * 128 : (j + 1) * 128] = lines_ref[
                    pl.ds(i * cols + me * share + j, 1), :
                ]

    for i in range(3):
        down(i)
        if i == 0 and t == 0:
            gain()
        back(i)
    for k, copy in enumerate(writes):
        if not merge or k != 1:
            copy.wait()


def token_step(t, at, toks, sources, shards, held, act, mul, h, hot, down, done):
    hidden, width = held.shape[1:]
    scen, count = hot.shape
    parts = len(shards)
    merge = t == toks - 1
    anywhere = pl.BlockSpec(memory_space=pltpu.HBM)
    vmem = pl.BlockSpec(memory_space=pltpu.VMEM)
    operands = list(shards) + [held, act, mul, h, hot]
    specs = [vmem] * (parts + 5)
    aliases = {}
    if t:
        aliases = {len(operands): 0, len(operands) + 1: 1}
        operands += list(down)
        specs += [anywhere, vmem]
    scratch = [
        pltpu.VMEM((count, width), BF16),
        pltpu.VMEM((hidden, width), BF16),
        pltpu.SemaphoreType.DMA((6,)),
    ]
    if merge:
        operands += list(done)
        specs += [vmem] * t
        scratch.append(pltpu.VMEM((2, count, toks, hidden // 3), BF16))
        gate_shape = (scen, toks, hidden)
    else:
        gate_shape = (scen, hidden)
    shapes = [
        jax.ShapeDtypeStruct((toks, hidden, width), BF16),
        jax.ShapeDtypeStruct((hidden // 128, count * toks, 128), F32),
        jax.ShapeDtypeStruct(gate_shape, F32),
    ]
    out_specs = [anywhere, vmem, vmem]
    if merge:
        shapes.append(jax.ShapeDtypeStruct((count, toks, hidden), BF16))
        out_specs.append(anywhere)
    if not t:
        shapes.append(jax.ShapeDtypeStruct((toks, width // parts), F32))
        out_specs.append(vmem)
        scratch.append(pltpu.VMEM((shards[0].shape[1], 128), F32))
    return pl.pallas_call(
        functools.partial(token_kernel, t, at, parts, merge, sources),
        in_specs=specs,
        out_specs=out_specs,
        scratch_shapes=scratch,
        out_shape=shapes,
        input_output_aliases=aliases,
        compiler_params=pltpu.CompilerParams(vmem_limit_bytes=14 << 20),
        cost_estimate=pl.CostEstimate(flops=1, bytes_accessed=1, transcendentals=0),
        name="token",
    )(*operands)


def plain_tokens(dz, pre_act, gates, down_weight, scenario):
    piece = lax.all_gather(dz, "dp", axis=1, tiled=True)
    onehot = (scenario[:, None] == jnp.arange(gates.shape[0], dtype=jnp.int32)[None, :]).astype(F32)
    rate = jnp.einsum("bs,stf->btf", onehot, gates, precision=lax.Precision.HIGHEST)
    activated, slope = gelu_parts(pre_act.astype(F32))
    hidden = (activated * rate).astype(BF16)
    d_hidden = jnp.einsum("tbc,tfc->btf", piece, down_weight, preferred_element_type=F32)
    gate = jnp.einsum("bs,btf->stf", onehot, d_hidden * activated, precision=lax.Precision.HIGHEST)
    pre = (d_hidden * rate * slope).astype(BF16)
    down = jnp.einsum("btf,tbc->tfc", hidden, piece, preferred_element_type=F32).astype(BF16)
    return pre, down, gate


def after(value, *others):
    return lax.optimization_barrier((value, *others))[0]


def swap(send):
    groups = 1 + len(send)
    return [
        lax.ppermute(v, "tok", [(p, p ^ (k + 1)) for p in range(groups)]) for k, v in enumerate(send)
    ]


def ring_tokens(dz, send, pre_act, gates, down_weight, scenario):
    dp = lax.axis_size("dp")
    order = ring_order(dp)
    ring = [(order[k], order[(k + 1) % dp]) for k in range(dp)]
    place = {device: k for k, device in enumerate(order)}
    sources = [[order[(place[m] - s) % dp] for s in range(dp)] for m in range(dp)]
    shards = [[v] for v in dz]

    def hop(i, *others):
        last = shards[i][-1]
        shards[i].append(lax.ppermute(after(last, *others) if others else last, "dp", ring))

    for i in range(4):
        hop(i)
    recv = swap(send)
    h, act, mul, held, hot, rest = [
        [v] for v in activations(0, pre_act, gates, scenario.reshape(1, -1), down_weight)
    ]
    hop(0, h[0])
    hop(1, h[0], shards[2][1])
    hot, rest = hot[0], rest[0]
    more = activations(2, rest, gates, hot, down_weight)
    for have, new in zip((h, act, mul, held), more):
        have.append(new)
    d_input = mix([after(r, h[0]) for r in recv], dz, down_weight.shape[2])
    hop(2, h[1])
    hop(3)
    hop(0)
    hop(1)
    hot = after(hot, d_input)

    down, rows, done = None, None, []
    homes = [(i, k) for i, v in enumerate(dz) for k in range(v.shape[0])]
    for t, (i, at) in enumerate(homes):
        down, rows, gate, *more = token_step(
            t, at, len(homes), sources, shards[i], held[t // 2], act[t // 2], mul[t // 2], h[t // 2], hot, (down, rows), done
        )
        done.append(gate)
        if t == 0:
            gain_gradient = more[0]
            hop(2, gate)
        if t == 1:
            hop(3, gate)
    return d_input, more[0], down, gate, gain_gradient


def per_device(pre_norm, cotangent, gain, pre_act, gates, down_weight, scenario):
    groups = lax.axis_size("tok")
    toks, width = gain.shape
    fits = down_weight.shape[1] == 1536 and toks == 4 and lax.axis_size("dp") == 4
    chunks, spare = ((1, 1, 1, 1), 256) if fits else ((toks,), 0)
    outs = norm(pre_norm, cotangent, gain, groups, chunks, spare)
    dz, send, gain_part = outs[: len(chunks)], outs[len(chunks) : -1], outs[-1]
    if fits:
        return ring_tokens(dz, send, pre_act, gates, down_weight, scenario)
    d_input = mix(swap(send), dz, width)
    pre, down, gate = plain_tokens(dz[0], pre_act, gates, down_weight, scenario)
    gain_gradient = lax.psum_scatter(gain_part, "dp", scatter_dimension=1, tiled=True)
    return d_input, pre, down, gate, gain_gradient


def solution(mesh):
    placed = (
        P(("group", "dp"), "tok", None),
        P(("group", "dp"), "tok", None),
        P("tok", None),
        P("group", "tok", "dp"),
        P(None, "tok", "dp"),
        P("tok", "dp", None),
        P("group"),
    )
    return jax.shard_map(
        per_device,
        mesh=mesh,
        in_specs=placed,
        out_specs=(
            P(("group", "dp"), "tok", None),
            P("group", "tok", "dp"),
            P(("group", "tok"), "dp", None),
            P("group", "tok", "dp"),
            P(("group", "tok"), "dp"),
        ),
        check_vma=False,
    )
```
